32 devices in a mesh: dp: 16 (over z, x, core), seq: 2 (over y).
Axes of the slice: x: 2, y: 2, z: 4, core: 2. Of those that a mesh axis runs over, the one named last changes fastest.
Arguments:
- tokens: bfloat16 [64, 1024, 1024], P('dp', 'seq'), may hold values from -6 to 6
- first_gain: bfloat16 [1024], P(('dp', 'seq')), may hold values from 0.25 to 1.75
- first_shift: bfloat16 [1024], P(('dp', 'seq')), may hold values from -1.75 to 1.75
- query_weight: bfloat16 [1024, 1024], P('dp', 'seq'), may hold values from -0.1875 to 0.1875
- query_bias: bfloat16 [1024], P(('dp', 'seq')), may hold values from -1.75 to 1.75
- key_weight: bfloat16 [1024, 1024], P('dp', 'seq'), may hold values from -0.1875 to 0.1875
- value_weight: bfloat16 [1024, 1024], P('dp', 'seq'), may hold values from -0.1875 to 0.1875
- value_bias: bfloat16 [1024], P(('dp', 'seq')), may hold values from -0.625 to 0.625
- output_weight: bfloat16 [1024, 1024], P('dp', 'seq'), may hold values from -0.375 to 0.375
- output_bias: bfloat16 [1024], P(('dp', 'seq')), may hold values from -1.75 to 1.75
- second_gain: bfloat16 [1024], P(('dp', 'seq')), may hold values from 0.25 to 1.75
- second_shift: bfloat16 [1024], P(('dp', 'seq')), may hold values from -1.75 to 1.75
- up_weight: bfloat16 [1024, 4096], P('dp', 'seq'), may hold values from -0.1875 to 0.1875
- up_bias: bfloat16 [4096], P(('dp', 'seq')), may hold values from -6 to 6
- down_weight: bfloat16 [4096, 1024], P('dp', 'seq'), may hold values from -0.09375 to 0.09375
- down_bias: bfloat16 [1024], P(('dp', 'seq')), may hold values from -1.75 to 1.75
- piece_starts: int32 [64, 2], P('dp'), may hold values from 0 to 768, as said below
- out_grad: bfloat16 [64, 1024, 1024], P('dp', 'seq'), may hold values from -6 to 6
Outputs:
- output: bfloat16 [64, 1024, 1024], P('dp', 'seq')
- input_grad: bfloat16 [64, 1024, 1024], P('dp', 'seq')
- first_gain_grad: float32 [1024], P(('dp', 'seq'))
- first_shift_grad: float32 [1024], P(('dp', 'seq'))
- query_weight_grad: float32 [1024, 1024], P('dp', 'seq')
- query_bias_grad: float32 [1024], P(('dp', 'seq'))
- key_weight_grad: float32 [1024, 1024], P('dp', 'seq')
- value_weight_grad: float32 [1024, 1024], P('dp', 'seq')
- value_bias_grad: float32 [1024], P(('dp', 'seq'))
- output_weight_grad: float32 [1024, 1024], P('dp', 'seq')
- output_bias_grad: float32 [1024], P(('dp', 'seq'))
- second_gain_grad: float32 [1024], P(('dp', 'seq'))
- second_shift_grad: float32 [1024], P(('dp', 'seq'))
- up_weight_grad: float32 [1024, 4096], P('dp', 'seq')
- up_bias_grad: float32 [4096], P(('dp', 'seq'))
- down_weight_grad: float32 [4096, 1024], P('dp', 'seq')
- down_bias_grad: float32 [1024], P(('dp', 'seq'))
The draws below stay inside these ranges and needn't reach their ends.
Inputs may be any that keep to these rules, and one draw needn't show every extreme that they name: `piece_starts`: each sequence holds two picture pieces of 256 tokens inside its 1024 tokens; the second starts at or after the end of the first.
All inputs are finite; a program needn't handle non-finite values.
Results may differ from the reference program's by a relative error of at most 0.024.
Values may be sent and summed in bfloat16 or wider, within the bound.
No kernel may reach another device: no remote copies, remote signals or barrier semaphores. Data moves between devices by JAX's collectives and lax.ppermute only.
A program may use at most 640 MiB of HBM per device.

```python
import jax
import jax.numpy as jnp
from jax import lax

D = 1024
HEADS = 16
HEAD_DIM = 64
FF = 4096
PIECE = 256
LEN = 1024
SEQUENCES = 64


def draw_piece_starts(key, part):
    room = LEN - 2 * PIECE
    split_keys = jax.random.split(key, 4)
    rows = jnp.arange(SEQUENCES, dtype=jnp.int32)
    before_second = jax.random.randint(split_keys[0], (SEQUENCES,), 0, room + 1)
    row_last = jax.random.randint(split_keys[1], (), 0, SEQUENCES)
    before_second = jnp.where(rows == row_last, room, before_second)
    opening = jax.random.randint(split_keys[2], (SEQUENCES,), 0, before_second + 1)
    row_first = jax.random.randint(split_keys[3], (), 0, SEQUENCES)
    opening = jnp.where(rows == row_first, 0, opening)
    return jnp.stack([opening, before_second + PIECE], axis=1).astype(jnp.int32)


def spiked(entries, key, source, target, shards_of, factor):
    def block_of(axis_at):
        return (jnp.arange(entries.shape[axis_at]) // (entries.shape[axis_at] // shards_of)).reshape((-1,) + (1,) * (entries.ndim - 1 - axis_at))

    one_side = jax.random.permutation(key, shards_of)[block_of(target)]
    other_side = (block_of(target) + shards_of // 2) % shards_of
    return jnp.where((block_of(source) == one_side) | (block_of(source) == other_side), factor * entries, entries)


def shard_levels(own_key, shape, cuts, low, high):
    gain = 1.0
    for position, blocks in cuts:
        draws = jax.random.uniform(jax.random.fold_in(jax.random.fold_in(own_key, 6), position), (blocks,), jnp.float32, low / len(cuts), high / len(cuts))
        gain = gain * jnp.repeat(jnp.exp(draws), shape[position] // blocks).reshape((-1,) + (1,) * (len(shape) - 1 - position))
    return gain


def centred(stream_key, extent, deviation, bound, cuts=(), held_as=jnp.bfloat16):
    level = shard_levels(stream_key, extent, cuts, -0.22, 0.18) if cuts else 1.0
    drawn = jax.random.normal(stream_key, extent, jnp.float32) * deviation * level
    return jnp.minimum(jnp.maximum(drawn, -bound), bound).astype(held_as)


def heavy_noise(rng, shape, scale, bound, cuts, heavy, kind=jnp.bfloat16):
    entries = scale * jax.random.normal(rng, shape, jnp.float32)
    if cuts:
        entries = entries * shard_levels(rng, shape, cuts, -0.22, 0.18)
    return jnp.clip(spiked(entries, jax.random.fold_in(rng, 3), *heavy), -bound, bound).astype(kind)


def setup_inputs(seed: int = 0) -> dict:
    seeds = jax.random.split(jax.random.key(seed), 19)
    tokens = heavy_noise(seeds[0], (SEQUENCES, LEN, D), 1.0, 6.0, ((0, 16), (1, 2)), (0, 2, 16, 2.0))
    first_gain = jnp.clip(1.0 + 0.15 * jax.random.normal(seeds[1], (D,), jnp.float32), 0.25, 1.75).astype(jnp.bfloat16)
    first_shift = centred(seeds[2], (D,), 0.3, 1.75, ((0, 32),))
    query_weight = centred(seeds[3], (D, D), D ** -0.5, 0.1875, ((0, 16), (1, 2)))
    query_bias = centred(seeds[4], (D,), 0.3, 1.75, ((0, 32),))
    key_weight = centred(seeds[5], (D, D), D ** -0.5, 0.1875, ((0, 16), (1, 2)))
    value_weight = centred(seeds[6], (D, D), D ** -0.5, 0.1875, ((0, 16), (1, 2)))
    value_bias = centred(seeds[7], (D,), 0.1, 0.625, ((0, 32),))
    output_weight = centred(seeds[8], (D, D), (min(D, max(D * 32 // LEN, D // 4))) ** -0.5, 0.375, ((0, 16), (1, 2)))
    output_bias = centred(seeds[9], (D,), 0.3, 1.75, ((0, 32),))
    second_gain = jnp.clip(1.0 + 0.15 * jax.random.normal(seeds[10], (D,), jnp.float32), 0.25, 1.75).astype(jnp.bfloat16)
    second_shift = centred(seeds[11], (D,), 0.3, 1.75, ((0, 32),))
    up_weight = centred(seeds[12], (D, FF), D ** -0.5, 0.1875, ((0, 16), (1, 2)))
    up_bias = centred(seeds[13], (FF,), 1.0, 6.0, ((0, 32),))
    down_weight = centred(seeds[14], (FF, D), FF ** -0.5, 0.09375, ((0, 16), (1, 2)))
    down_bias = centred(seeds[15], (D,), 0.3, 1.75, ((0, 32),))
    piece_starts = draw_piece_starts(jax.random.fold_in(seeds[18], 71), 0)
    out_grad = heavy_noise(seeds[17], (SEQUENCES, LEN, D), 1.0, 6.0, ((0, 16), (1, 2)), (0, 2, 16, 2.0))
    return {"tokens": tokens, "first_gain": first_gain, "first_shift": first_shift, "query_weight": query_weight, "query_bias": query_bias, "key_weight": key_weight, "value_weight": value_weight, "value_bias": value_bias, "output_weight": output_weight, "output_bias": output_bias, "second_gain": second_gain, "second_shift": second_shift, "up_weight": up_weight, "up_bias": up_bias, "down_weight": down_weight, "down_bias": down_bias, "piece_starts": piece_starts, "out_grad": out_grad}


@jax.custom_vjp
def low(v):
    return lax.optimization_barrier(v.astype(jnp.bfloat16)).astype(jnp.float32)

@jax.custom_vjp
def low_back(v):
    return v

def low_keep(v):
    return (low(v), None)

def low_pass(kept, grad):
    return (grad,)

def back_keep(v):
    return (v, None)

def back_low(kept, grad):
    return (low(grad),)
low.defvjp(low_keep, low_pass)
low_back.defvjp(back_keep, back_low)
HIGHEST = lax.Precision.HIGHEST
NEGATIVE = -1e+30
EPSILON = 1e-05

def layer_norm(values, scale_row, shift_row):
    centre = values - lax.optimization_barrier(jnp.mean(values, axis=-1, keepdims=True))
    spread = lax.optimization_barrier(jnp.mean(centre * centre, axis=-1, keepdims=True))
    return centre * lax.rsqrt(spread + EPSILON) * scale_row + shift_row

def piece_index(positions, starts):
    inside_first = (positions >= starts[0]) & (positions < starts[0] + PIECE)
    inside_second = (positions >= starts[1]) & (positions < starts[1] + PIECE)
    return jnp.where(inside_first, 0, jnp.where(inside_second, 1, -1))

def visible_pairs(starts):
    places = jnp.arange(LEN, dtype=jnp.int32)
    pieces = piece_index(places, starts)
    causal = places[None, :] <= places[:, None]
    joined = (pieces[:, None] == pieces[None, :]) & (pieces[:, None] >= 0)
    return causal | joined

def matmul(left_side, right_side):
    return jnp.dot(left_side, right_side, precision=HIGHEST)

def layer(inputs, params, starts):
    first_gain, first_shift, query_weight, query_bias, key_weight, value_weight, value_bias, output_weight, output_bias, second_gain, second_shift, up_weight, up_bias, down_weight, down_bias = params
    normed = low(layer_norm(inputs, first_gain, first_shift))
    queries = low(low_back(matmul(normed, query_weight) + query_bias)).reshape(LEN, HEADS, HEAD_DIM)
    key_rows = low(low_back(matmul(normed, key_weight))).reshape(LEN, HEADS, HEAD_DIM)
    value_rows = low(low_back(matmul(normed, value_weight) + value_bias)).reshape(LEN, HEADS, HEAD_DIM)
    scores = low_back(jnp.einsum('qhd,khd->hqk', queries, key_rows, precision=HIGHEST) * HEAD_DIM ** (-0.5))
    scores = jnp.where(visible_pairs(starts)[None], scores, NEGATIVE)
    highest = lax.optimization_barrier(jnp.max(scores, axis=-1, keepdims=True))
    raised = jnp.exp(scores - highest)
    softened = raised / lax.optimization_barrier(jnp.sum(raised, axis=-1, keepdims=True))
    attended = jnp.einsum('hqk,khd->qhd', low(softened), value_rows, precision=HIGHEST).reshape(LEN, HEADS * HEAD_DIM)
    attended = low(low_back(attended))
    middle = inputs + low_back(matmul(attended, output_weight) + output_bias)
    second = low(layer_norm(middle, second_gain, second_shift))
    active = low(jax.nn.gelu(low_back(matmul(second, up_weight) + up_bias), approximate=True))
    return middle + low_back(matmul(active, down_weight) + down_bias)

def reference(tokens, first_gain, first_shift, query_weight, query_bias, key_weight, value_weight, value_bias, output_weight, output_bias, second_gain, second_shift, up_weight, up_bias, down_weight, down_bias, piece_starts, out_grad):
    params = tuple((weight.astype(jnp.float32) for weight in (first_gain, first_shift, query_weight, query_bias, key_weight, value_weight, value_bias, output_weight, output_bias, second_gain, second_shift, up_weight, up_bias, down_weight, down_bias)))
    zeroed = tuple((jnp.zeros_like(weight) for weight in params))

    def one_sequence(running, sequence_item):
        inputs, starts, incoming = sequence_item
        result, pullback = jax.vjp(lambda source, weights: layer(source, weights, starts), inputs, params)
        input_grad, weight_grads = pullback(incoming)
        running = tuple((earlier + summand for earlier, summand in zip(running, weight_grads)))
        return (running, (result.astype(jnp.bfloat16), input_grad.astype(jnp.bfloat16)))
    totals, (output, input_grad) = lax.scan(one_sequence, zeroed, (tokens.astype(jnp.float32), piece_starts, out_grad.astype(jnp.float32)))
    return (output, input_grad, totals[0], totals[1], totals[2], totals[3], totals[4], totals[5], totals[6], totals[7], totals[8], totals[9], totals[10], totals[11], totals[12], totals[13], totals[14])
```

```python
import functools
import math

import jax
import jax.numpy as jnp
from jax import lax
from jax.experimental import pallas as pl
from jax.experimental.pallas import tpu as pltpu
from jax.sharding import Mesh, PartitionSpec as P

HEAD_DIM = 64
PIECE = 256
NEGATIVE = -1e30
EPSILON = 1e-05
BENDING = math.sqrt(2.0 / math.pi)
CUBIC_TERM = 0.044715
SCALE = HEAD_DIM**-0.5
LOG2E = math.log2(math.e)

BF = jnp.bfloat16
F32 = jnp.float32
VMEM_LIMIT = 60 * 2**20

NN = (((1,), (0,)), ((), ()))
NT = (((1,), (1,)), ((), ()))
TN = (((0,), (0,)), ((), ()))


def dot(left, right, form):
    return lax.dot_general(left, right, form, preferred_element_type=F32)


def params():
    return pltpu.CompilerParams(vmem_limit_bytes=VMEM_LIMIT)


def cost(flops, nbytes, trans=0):
    return pl.CostEstimate(flops=int(flops), bytes_accessed=int(nbytes), transcendentals=int(trans))


def shape(dims, dtype):
    return jax.ShapeDtypeStruct(dims, dtype)


def once(block, index):
    return pl.BlockSpec(block, index, pipeline_mode=pl.Buffered(1))


def after(values, *earlier):
    return lax.optimization_barrier((values,) + earlier)[0]


def norm_parts(values):
    centre = values - jnp.mean(values, axis=-1, keepdims=True)
    inverse = lax.rsqrt(jnp.mean(centre * centre, axis=-1, keepdims=True) + EPSILON)
    return centre * inverse, inverse


def norm_back(upstream, hat, inverse, gain):
    scaled = upstream * gain
    return inverse * (
        scaled
        - jnp.mean(scaled, axis=-1, keepdims=True)
        - hat * jnp.mean(scaled * hat, axis=-1, keepdims=True)
    )


def fold(values):
    rows, columns = values.shape
    return jnp.sum(values.reshape(rows // 8, 8, columns), axis=0)


def accumulate(ref, values):
    @pl.when(pl.program_id(0) == 0)
    def _():
        ref[...] = values

    @pl.when(pl.program_id(0) > 0)
    def _():
        ref[...] += values


GAIN_ONE, SHIFT_ONE, QUERY_BIAS, VALUE_BIAS, OUTPUT_BIAS, GAIN_TWO, SHIFT_TWO, DOWN_BIAS = range(8)


def row(ref, index):
    return ref[index : index + 1, :]


def weight_columns(ref, j, rows=slice(None)):
    block = ref[:, j, rows, :]
    return block.reshape(block.shape[0] * block.shape[1], block.shape[2])


def project_body(x_ref, vec_ref, w_ref, x1_ref, q_ref, k_ref, v_ref):
    hat, _ = norm_parts(x_ref[...].astype(F32))
    x1 = (hat * row(vec_ref, GAIN_ONE) + row(vec_ref, SHIFT_ONE)).astype(BF)
    x1_ref[...] = x1
    groups, per, width = w_ref.shape[1], w_ref.shape[2] // 3, w_ref.shape[3]
    for m, (out, bias) in enumerate(((q_ref, QUERY_BIAS), (k_ref, None), (v_ref, VALUE_BIAS))):
        for j in range(groups):
            at = slice(j * width, (j + 1) * width)
            y = dot(x1, weight_columns(w_ref, j, slice(m * per, (m + 1) * per)), NN)
            if bias is not None:
                y = y + vec_ref[bias : bias + 1, at]
            out[:, at] = y.astype(BF)


def project(x, vec, first, tile):
    tokens, d = x.shape
    dp, g, rows, width = first.shape
    per = d // dp
    tok = pl.BlockSpec((tile, d), lambda i: (i, 0))
    return pl.pallas_call(
        project_body,
        grid=(tokens // tile,),
        in_specs=[tok, once((8, d), lambda i: (0, 0)), once((dp, g, 3 * per, width), lambda i: (0, 0, 0, 0))],
        out_specs=[tok] * 4,
        out_shape=[shape((tokens, d), BF)] * 4,
        compiler_params=params(),
        cost_estimate=cost(6 * tokens * d * d, 10 * tokens * d + 6 * d * d),
        name="project",
    )(x, vec, first)


def reach_of(places, first, second):
    in_first = (places >= first) & (places < first + PIECE)
    in_second = (places >= second) & (places < second + PIECE)
    return jnp.where(in_first, first + (PIECE - 1), jnp.where(in_second, second + (PIECE - 1), places))


def query_blocks(starts_ref, offset_ref, queries, keys, fixed_offset, run):
    b = pl.program_id(0)
    first, second = starts_ref[b, 0], starts_ref[b, 1]
    offset = offset_ref[0]
    block = min(256, queries)
    for n in range(queries // block):
        begin = offset + n * block
        last = reach_of(begin + (block - 1), first, second)
        places = begin + lax.broadcasted_iota(jnp.int32, (1, block), 1)
        reach = reach_of(places, first, second)
        if fixed_offset:
            options = range(n + 1, min(n + 2, keys // 256) + 1)
        else:
            options = range(1, keys // 256 + 1)
        for tiles in options:
            clear = n if fixed_offset else 0

            @pl.when((last >= (tiles - 1) * 256) & (last < tiles * 256))
            def _(n=n, tiles=tiles, clear=clear, reach=reach):
                run(slice(n * block, (n + 1) * block), clear * 256, tiles * 256, reach)


def hide(scores, clear, reach):
    span, block = scores.shape
    places = clear + lax.broadcasted_iota(jnp.int32, (span - clear, block), 0)
    tail = jnp.where(places <= reach, scores[clear:], NEGATIVE)
    return tail if clear == 0 else jnp.concatenate([scores[:clear], tail], axis=0)


def head_masks():
    lanes = lax.broadcasted_iota(jnp.int32, (1, 2 * HEAD_DIM), 1)
    return [lanes < HEAD_DIM, lanes >= HEAD_DIM]


def pick(mask, values):
    return jnp.where(mask, values, jnp.zeros_like(values))


def attend_body(fixed_offset, starts_ref, offset_ref, q_ref, k_ref, v_ref, out_ref, lse_ref):
    masks = head_masks()
    queries, keys = q_ref.shape[1], k_ref.shape[1]

    def run(at, clear, span, reach):
        q = q_ref[0, at, :]
        k = k_ref[0, :span, :]
        v = v_ref[0, :span, :]
        total = None
        scales = []
        for h in range(2):
            s = hide(dot(k, pick(masks[h], q), NT), clear, reach)
            top = jnp.max(s, axis=0, keepdims=True)
            p = jnp.exp2((s - top) * (SCALE * LOG2E))
            size = jnp.sum(p, axis=0, keepdims=True)
            lse_ref[0, 0, h : h + 1, at] = top * (SCALE * LOG2E) + jnp.log2(size)
            scales.append(1.0 / size)
            part = dot(pick(masks[h], v), p.astype(BF), TN)
            total = part if total is None else total + part
        half = HEAD_DIM
        out_ref[:half, at] = (total[:half] * scales[0]).astype(BF)
        out_ref[half:, at] = (total[half:] * scales[1]).astype(BF)

    query_blocks(starts_ref, offset_ref, queries, keys, fixed_offset, run)


def attend(starts, offset, q, k, v, fixed_offset):
    count, queries, d = q.shape
    keys = k.shape[1]
    pairs = d // 128
    rows = lambda n: pl.BlockSpec((1, n, 128), lambda b, p, *_: (b, 0, p))
    return pl.pallas_call(
        functools.partial(attend_body, fixed_offset),
        grid_spec=pltpu.PrefetchScalarGridSpec(
            num_scalar_prefetch=2,
            grid=(count, pairs),
            in_specs=[rows(queries), rows(keys), rows(keys)],
            out_specs=[
                pl.BlockSpec((128, queries), lambda b, p, *_: (p, b)),
                pl.BlockSpec((1, 1, 2, queries), lambda b, p, *_: (b, p, 0, 0)),
            ],
        ),
        out_shape=[shape((d, count * queries), BF), shape((count, pairs, 2, queries), F32)],
        compiler_params=params(),
        cost_estimate=cost(12 * count * queries * keys * d, 8 * count * keys * d, count * pairs * 2 * queries * keys),
        name="attend",
    )(starts, offset, q, k, v)


def attend_back_body(
    fixed_offset, starts_ref, offset_ref, q_ref, k_ref, v_ref, g_ref, lse_ref, dq_ref, dkv_ref, dk_acc, dv_acc
):
    masks = head_masks()
    queries, keys = q_ref.shape[1], k_ref.shape[1]
    dk_acc[...] = jnp.zeros_like(dk_acc)
    dv_acc[...] = jnp.zeros_like(dv_acc)

    def run(at, clear, span, reach):
        q = q_ref[0, at, :]
        g = g_ref[0, at, :]
        k = k_ref[0, :span, :]
        v = v_ref[0, :span, :]
        dq = None
        chances, slopes, qs, gs = [], [], [], []
        for h in range(2):
            qh, gh = pick(masks[h], q), pick(masks[h], g)
            s = hide(dot(k, qh, NT), clear, reach)
            p = jnp.exp2(s * (SCALE * LOG2E) - lse_ref[0, 0, h : h + 1, at])
            dp = dot(v, gh, NT)
            settled = jnp.sum(p * dp, axis=0, keepdims=True)
            ds = (p * (dp - settled)).astype(BF)
            part = dot(pick(masks[h], k), ds, TN)
            dq = part if dq is None else dq + part
            chances.append(p.astype(BF))
            slopes.append(ds)
            qs.append(qh)
            gs.append(gh)
        dv_acc[:span, :] += dot(jnp.concatenate(chances, axis=1), jnp.concatenate(gs, axis=0), NN)
        dk_acc[:span, :] += dot(jnp.concatenate(slopes, axis=1), jnp.concatenate(qs, axis=0), NN)
        dq_ref[0, at, :] = (dq.T * SCALE).astype(BF)

    query_blocks(starts_ref, offset_ref, queries, keys, fixed_offset, run)
    dkv_ref[0, 0] = (dk_acc[...] * SCALE).astype(BF)
    dkv_ref[1, 0] = dv_acc[...].astype(BF)


def attend_back(starts, offset, q, k, v, g, lse, fixed_offset):
    count, queries, d = q.shape
    keys = k.shape[1]
    pairs = d // 128
    rows = lambda n: pl.BlockSpec((1, n, 128), lambda b, p, *_: (b, 0, p))
    return pl.pallas_call(
        functools.partial(attend_back_body, fixed_offset),
        grid_spec=pltpu.PrefetchScalarGridSpec(
            num_scalar_prefetch=2,
            grid=(count, pairs),
            in_specs=[
                rows(queries),
                rows(keys),
                rows(keys),
                rows(queries),
                pl.BlockSpec((1, 1, 2, queries), lambda b, p, *_: (b, p, 0, 0)),
            ],
            out_specs=[
                rows(queries),
                pl.BlockSpec((2, 1, keys, 128), lambda b, p, *_: (0, b, 0, p)),
            ],
            scratch_shapes=[pltpu.VMEM((keys, 128), F32)] * 2,
        ),
        out_shape=[shape((count, queries, d), BF), shape((2, count, keys, d), BF)],
        compiler_params=params(),
        cost_estimate=cost(30 * count * queries * keys * d, 14 * count * keys * d, count * pairs * 2 * queries * keys),
        name="attend_back",
    )(starts, offset, q, k, v, g, lse)


def hidden_chunk(up_ref):
    return min(512, up_ref.shape[3])


def up_chunk(up_ref, n, size):
    per = up_ref.shape[3] // size
    block = up_ref[:, n // per, :, (n % per) * size : (n % per + 1) * size]
    return block.reshape(block.shape[0] * block.shape[1], size)


def rise_body(x_ref, att_ref, vec_ref, upb_ref, wo_ref, up_ref, mid_ref, x2_ref, act_ref, slope_ref):
    att = att_ref[...]
    width = wo_ref.shape[3]
    parts = [dot(att, weight_columns(wo_ref, j), TN) for j in range(wo_ref.shape[1])]
    branch = jnp.concatenate(parts, axis=1)
    middle = x_ref[...].astype(F32) + (branch + row(vec_ref, OUTPUT_BIAS))
    mid_ref[...] = middle
    hat, _ = norm_parts(middle)
    x2 = (hat * row(vec_ref, GAIN_TWO) + row(vec_ref, SHIFT_TWO)).astype(BF)
    x2_ref[...] = x2
    size = hidden_chunk(up_ref)
    for n in range(up_ref.shape[1] * up_ref.shape[3] // size):
        at = slice(n * size, (n + 1) * size)
        x = dot(x2, up_chunk(up_ref, n, size), NN) + upb_ref[:, at]
        square = x * x
        t = jnp.tanh(x * (BENDING + (BENDING * CUBIC_TERM) * square))
        half = 0.5 * (1.0 + t)
        act_ref[:, at] = (x * half).astype(BF)
        bend = (0.5 * BENDING) * x * (1.0 + (3.0 * CUBIC_TERM) * square)
        slope_ref[:, at] = (half + bend * (1.0 - t * t)).astype(BF)


def rise(x, att, vec, upb, first, up, tile):
    tokens, d = x.shape
    dp, g, _, width = first.shape
    per = d // dp
    ff = upb.shape[1]
    tok = pl.BlockSpec((tile, d), lambda i: (i, 0))
    wide = pl.BlockSpec((tile, ff), lambda i: (i, 0))
    return pl.pallas_call(
        rise_body,
        grid=(tokens // tile,),
        in_specs=[
            tok,
            pl.BlockSpec((d, tile), lambda i: (0, i)),
            once((8, d), lambda i: (0, 0)),
            once((1, ff), lambda i: (0, 0)),
            once((dp, g, per, width), lambda i: (0, 0, 3, 0)),
            once(up.shape, lambda i: (0, 0, 0, 0)),
        ],
        out_specs=[tok, tok, wide, wide],
        out_shape=[shape((tokens, d), F32), shape((tokens, d), BF), shape((tokens, ff), BF), shape((tokens, ff), BF)],
        compiler_params=params(),
        cost_estimate=cost(2 * tokens * d * (d + ff), tokens * (10 * d + 4 * ff) + 2 * d * (d + ff), tokens * ff),
        name="rise",
    )(x, att, vec, upb, first, up)


def fall_body(
    mid_ref, act_ref, slope_ref, og_ref, vec_ref, wo_ref, up_ref, down_ref,
    out_ref, bg_ref, mg_ref, br_ref, dat_ref, upb_ref, sums_ref,
):
    og = og_ref[...]
    incoming = og.astype(F32)
    g, width = down_ref.shape[1], down_ref.shape[3]
    size = hidden_chunk(up_ref)
    per = size // down_ref.shape[2]
    chunks = up_ref.shape[1] * up_ref.shape[3] // size
    outs = [None] * g
    e = None
    for n in range(chunks):
        at = slice(n * size, (n + 1) * size)
        act = act_ref[:, at]
        rise_grad = None
        for j in range(g):
            block = down_ref[n * per : (n + 1) * per, j].reshape(size, width)
            part = dot(og[:, j * width : (j + 1) * width], block, NT)
            rise_grad = part if rise_grad is None else rise_grad + part
            part = dot(act, block, NN)
            outs[j] = part if outs[j] is None else outs[j] + part
        bg = (slope_ref[:, at].astype(F32) * rise_grad).astype(BF)
        bg_ref[:, at] = bg
        accumulate(upb_ref.at[:, at], fold(bg.astype(F32)))
        part = dot(bg, up_chunk(up_ref, n, size), NT)
        e = part if e is None else e + part
    middle = mid_ref[...]
    out_ref[...] = (middle + (jnp.concatenate(outs, axis=1) + row(vec_ref, DOWN_BIAS))).astype(BF)
    hat, inverse = norm_parts(middle)
    middle_grad = incoming + norm_back(e, hat, inverse, row(vec_ref, GAIN_TWO))
    mg_ref[...] = middle_grad
    branch = middle_grad.astype(BF)
    br_ref[...] = branch
    back = None
    for j in range(wo_ref.shape[1]):
        part = dot(branch[:, j * width : (j + 1) * width], weight_columns(wo_ref, j), NT)
        back = part if back is None else back + part
    dat_ref[...] = back.astype(BF)
    accumulate(sums_ref.at[0], fold(e * hat))
    accumulate(sums_ref.at[1], fold(e))
    accumulate(sums_ref.at[2], fold(branch.astype(F32)))
    accumulate(sums_ref.at[3], fold(incoming))


def fall(middle, act, slope, og, vec, first, up, down, tile):
    tokens, d = og.shape
    dp, g, _, width = first.shape
    per = d // dp
    ff = act.shape[1]
    tok = pl.BlockSpec((tile, d), lambda i: (i, 0))
    wide = pl.BlockSpec((tile, ff), lambda i: (i, 0))
    return pl.pallas_call(
        fall_body,
        grid=(tokens // tile,),
        in_specs=[
            tok, wide, wide, tok,
            once((8, d), lambda i: (0, 0)),
            once((dp, g, per, width), lambda i: (0, 0, 3, 0)),
            once(up.shape, lambda i: (0, 0, 0, 0)),
            once(down.shape, lambda i: (0, 0, 0, 0)),
        ],
        out_specs=[
            tok, wide, tok, tok, tok,
            pl.BlockSpec((8, ff), lambda i: (0, 0)),
            pl.BlockSpec((4, 8, d), lambda i: (0, 0, 0)),
        ],
        out_shape=[
            shape((tokens, d), BF), shape((tokens, ff), BF), shape((tokens, d), F32), shape((tokens, d), BF),
            shape((tokens, d), BF), shape((8, ff), F32), shape((4, 8, d), F32),
        ],
        compiler_params=params(),
        cost_estimate=cost(2 * tokens * d * (d + 3 * ff), tokens * (16 * d + 6 * ff) + 2 * d * (d + 2 * ff)),
        name="fall",
    )(middle, act, slope, og, vec, first, up, down)


def split_cores(core_ref, values, keep_ref, send_ref):
    even, odd = values[:, 0], values[:, 1]
    mine = core_ref[0] == 0
    keep_ref[...] = jnp.where(mine, even, odd).astype(BF)
    send_ref[...] = jnp.where(mine, odd, even).astype(BF)


def down_grad_body(core_ref, act_ref, og_ref, keep_ref, send_ref):
    y = dot(act_ref[...], og_ref[...], TN)
    chips, g, rows, width = keep_ref.shape
    for j in range(g):
        part = y[:, j * width : (j + 1) * width].reshape(chips, 2, rows, width)
        split_cores(core_ref, part, keep_ref.at[:, j], send_ref.at[:, j])


def down_grad(core, act, og, dp, g):
    tokens, ff = act.shape
    d = og.shape[1]
    size = min(512, ff)
    rows, width = ff // dp, d // g
    chips = size // rows // 2
    out = pl.BlockSpec((chips, g, rows, width), lambda i, *_: (i, 0, 0, 0))
    return pl.pallas_call(
        down_grad_body,
        grid_spec=pltpu.PrefetchScalarGridSpec(
            num_scalar_prefetch=1,
            grid=(ff // size,),
            in_specs=[pl.BlockSpec((tokens, size), lambda i, *_: (0, i)), once((tokens, d), lambda i, *_: (0, 0))],
            out_specs=[out, out],
        ),
        out_shape=[shape((dp // 2, g, rows, width), BF)] * 2,
        compiler_params=params(),
        cost_estimate=cost(2 * tokens * d * ff, 2 * (tokens * (d + ff) + d * ff)),
        name="down_grad",
    )(core, act, og)


def weight_grad_body(form, core_ref, x_ref, dy_ref, keep_ref, send_ref):
    dy = dy_ref[...]
    y = dot(x_ref[...], dy.reshape(dy.shape[-2:]), form)
    chips, _, rows, width = keep_ref.shape
    split_cores(core_ref, y.reshape(chips, 2, rows, width), keep_ref.at[:, 0], send_ref.at[:, 0])


def weight_grad(core, x, dy, dp, g, form, name):
    count, tokens, columns = dy.shape
    d = x.shape[0] if form == NN else x.shape[1]
    share = columns // g
    size = min(512, share)
    per = share // size
    rows = d // dp
    out = pl.BlockSpec((dp // 2, 1, rows, size), lambda m, i, *_: (0, i // per, m, i % per))
    return pl.pallas_call(
        functools.partial(weight_grad_body, form),
        grid_spec=pltpu.PrefetchScalarGridSpec(
            num_scalar_prefetch=1,
            grid=(count, columns // size),
            in_specs=[
                once(x.shape, lambda m, i, *_: (0, 0)),
                pl.BlockSpec((1, tokens, size), lambda m, i, *_: (m, 0, i)),
            ],
            out_specs=[out, out],
        ),
        out_shape=[shape((dp // 2, g, count * rows, share), BF)] * 2,
        compiler_params=params(),
        cost_estimate=cost(2 * count * tokens * d * columns, 2 * (tokens * d + count * columns * (tokens + d))),
        name=name,
    )(core, x, dy)


def input_body(x_ref, mg_ref, dq_ref, dkv_ref, vec_ref, w_ref, out_ref, sums_ref):
    groups, per, width = w_ref.shape[1], w_ref.shape[2] // 3, w_ref.shape[3]
    e = None
    grads = (dq_ref[...], dkv_ref[0], dkv_ref[1])
    for m in range(3):
        for j in range(groups):
            at = slice(j * width, (j + 1) * width)
            part = dot(grads[m][:, at], weight_columns(w_ref, j, slice(m * per, (m + 1) * per)), NT)
            e = part if e is None else e + part
    hat, inverse = norm_parts(x_ref[...].astype(F32))
    out_ref[...] = (mg_ref[...] + norm_back(e, hat, inverse, row(vec_ref, GAIN_ONE))).astype(BF)
    accumulate(sums_ref.at[0], fold(e * hat))
    accumulate(sums_ref.at[1], fold(e))
    accumulate(sums_ref.at[2], fold(grads[0].astype(F32)))
    accumulate(sums_ref.at[3], fold(grads[2].astype(F32)))


def input_back(x, mg, dq, dkv, vec, first, tile):
    tokens, d = x.shape
    dp, g, rows, width = first.shape
    per = d // dp
    tok = pl.BlockSpec((tile, d), lambda i: (i, 0))
    return pl.pallas_call(
        input_body,
        grid=(tokens // tile,),
        in_specs=[
            tok, tok, tok,
            pl.BlockSpec((2, tile, d), lambda i: (0, i, 0)),
            once((8, d), lambda i: (0, 0)),
            once((dp, g, 3 * per, width), lambda i: (0, 0, 0, 0)),
        ],
        out_specs=[tok, pl.BlockSpec((4, 8, d), lambda i: (0, 0, 0))],
        out_shape=[shape((tokens, d), BF), shape((4, 8, d), F32)],
        compiler_params=params(),
        cost_estimate=cost(6 * tokens * d * d, 16 * tokens * d + 6 * d * d),
        name="input_back",
    )(x, mg, dq, dkv, vec, first)


def swap_cores(values):
    return lax.ppermute(values, "core", [(0, 1), (1, 0)])


def add_cores(keep, send):
    return (keep.astype(F32) + swap_cores(send).astype(F32)).astype(BF)


def add_chips(mine):
    chips, g = mine.shape[:2]
    flat = mine.reshape((chips * g,) + mine.shape[2:])
    return lax.psum_scatter(flat, ("z", "x", "seq"), scatter_dimension=0, tiled=True)[0].astype(F32)


NEAR = ("z", [(0, 1), (1, 0), (2, 3), (3, 2)])
FAR = ("z", [(0, 2), (2, 0), (1, 3), (3, 1)])
ACROSS = ("x", [(0, 1), (1, 0)])
ALONG = ("seq", [(0, 1), (1, 0)])


def halve(values, dim, own, route):
    keep = lax.dynamic_index_in_dim(values, own, dim, keepdims=False)
    send = lax.dynamic_index_in_dim(values, 1 - own, dim, keepdims=False)
    return (keep.astype(F32) + lax.ppermute(send, *route).astype(F32)).astype(BF)


def add_chips_stepwise(mine, across_first):
    z, x, y = (lax.axis_index(name) for name in ("z", "x", "seq"))
    values = mine.reshape((2, 2, 2) + mine.shape[1:])
    if across_first:
        values = halve(values, 2, x, ACROSS)
    values = halve(values, 1, z % 2, NEAR)
    values = halve(values, 0, z // 2, FAR)
    if not across_first:
        values = halve(values, 0, x, ACROSS)
    return halve(values, 0, y, ALONG).astype(F32)


def body(
    tokens, first_gain, first_shift, query_weight, query_bias, key_weight, value_weight, value_bias,
    output_weight, output_bias, second_gain, second_shift, up_weight, up_bias, down_weight, down_bias,
    piece_starts, out_grad,
):
    chips, g = lax.axis_size("z") * lax.axis_size("x"), lax.axis_size("seq")
    dp = 2 * chips
    everyone = ("z", "x", "core", "seq")
    count, local, d = tokens.shape
    width = query_weight.shape[1]
    per = query_weight.shape[0]
    small = first_gain.shape[0]
    wide = up_bias.shape[0]
    ff = wide * dp * g
    length = local * g
    place = lax.axis_index("seq")
    core = lax.axis_index("core").astype(jnp.int32).reshape(1)
    paired = g == 2 and count % 2 == 0

    vectors = jnp.concatenate(
        [first_gain, first_shift, query_bias, value_bias, output_bias, second_gain, second_shift, down_bias, up_bias]
    )
    extra = -(-vectors.shape[0] // (16 * width)) * 16
    vectors = jnp.pad(vectors, (0, extra * width - vectors.shape[0])).reshape(extra, width)
    packed = jnp.concatenate([query_weight, key_weight, value_weight, output_weight, vectors], axis=0)
    first = lax.all_gather(packed, everyone, axis=0).reshape(dp, g, 4 * per + extra, width)
    up = lax.all_gather(up_weight, everyone, axis=0).reshape((dp, g) + up_weight.shape)
    down = lax.all_gather(down_weight, everyone, axis=0).reshape((dp, g) + down_weight.shape)

    flat = first[:, :, 4 * per :, :].reshape(dp * g, extra * width)[:, : 8 * small + wide].astype(F32)
    vec = flat[:, : 8 * small].reshape(dp * g, 8, small).transpose(1, 0, 2).reshape(8, d)
    upb = flat[:, 8 * small :].reshape(1, ff)

    if paired:
        half = count // 2

        def gather_rows(values):
            kept = lax.dynamic_slice_in_dim(values, place * half, half, 0)
            sent = lax.dynamic_slice_in_dim(values, (1 - place) * half, half, 0)
            came = lax.ppermute(sent, "seq", [(0, 1), (1, 0)])
            low = jnp.where(place == 0, kept, came)
            high = jnp.where(place == 0, came, kept)
            return jnp.concatenate([low, high], axis=1).reshape(half * length, d)

        def return_rows(values):
            values = values.reshape(half, 2, local, d)
            kept = lax.dynamic_index_in_dim(values, place, 1, keepdims=False)
            sent = lax.dynamic_index_in_dim(values, 1 - place, 1, keepdims=False)
            came = lax.ppermute(sent, "seq", [(0, 1), (1, 0)])
            low = jnp.where(place == 0, kept, came)
            high = jnp.where(place == 0, came, kept)
            return jnp.concatenate([low, high], axis=0)

        starts = lax.dynamic_slice_in_dim(piece_starts, place * half, half, 0)
        offset = jnp.zeros((1,), jnp.int32)
        sequences, queries = half, length
    else:
        gather_rows = lambda values: values.reshape(count * local, d)
        return_rows = lambda values: values.reshape(count, local, d)
        starts = piece_starts
        offset = (place * local).astype(jnp.int32).reshape(1)
        sequences, queries = count, local

    rows = sequences * queries
    tile = min(256, rows)
    x = gather_rows(tokens)
    og = gather_rows(after(out_grad, first))
    x1, q, k, v = project(x, vec, first, tile)
    q, k, v = (t.reshape(sequences, queries, d) for t in (q, k, v))
    if not paired:
        k, v = (lax.all_gather(t, "seq", axis=1, tiled=True) for t in (k, v))
    att, lse = attend(starts, offset, q, k, v, paired)
    middle, x2, act, slope = rise(x, att, vec, upb, first, up, tile)
    down_mine = add_cores(*down_grad(core, act, og, dp, g))
    down_sum = add_chips(down_mine)
    act = after(act, down_mine)
    out, bg, mg, branch, dat, upb_sums, sums_two = fall(middle, act, slope, og, vec, first, up, down, tile)
    output = return_rows(out)
    up_parts = weight_grad(core, x2, bg[None], dp, g, TN, "up_grad")
    out_parts = weight_grad(core, att, branch[None], dp, g, NN, "out_grad")
    up_mine = jnp.concatenate([add_cores(*up_parts), add_cores(*out_parts)], axis=-1)
    up_sum = add_chips(up_mine)
    dat = after(dat, up_mine, down_sum)
    dq, dkv = attend_back(starts, offset, q, k, v, dat.reshape(sequences, queries, d), lse, paired)
    dq = after(dq.reshape(rows, d), output)
    if not paired:
        dkv = lax.psum_scatter(dkv, "seq", scatter_dimension=2, tiled=True)
    dkv = dkv.reshape(2, rows, d)
    query_parts = weight_grad(core, x1, dq[None], dp, g, TN, "query_grad")
    kv_parts = weight_grad(core, x1, dkv, dp, g, TN, "key_value_grad")
    matrix_mine = jnp.concatenate([add_cores(*query_parts), add_cores(*kv_parts)], axis=2)
    in_grad, sums_one = input_back(x, mg, dq, after(dkv, matrix_mine, up_sum), vec, first, tile)
    input_grad = return_rows(in_grad)

    one, two = jnp.sum(sums_one, axis=1), jnp.sum(sums_two, axis=1)
    eight = jnp.stack([one[0], one[1], one[2], one[3], two[2], two[0], two[1], two[3]])
    eight = eight.reshape(8, chips, 2, g, small).transpose(2, 1, 3, 0, 4).reshape(2, chips, g, 8 * small)
    upb_grad = jnp.sum(upb_sums, axis=0).reshape(chips, 2, g, wide).transpose(1, 0, 2, 3)
    lines = jnp.concatenate([eight, upb_grad], axis=-1)
    lines = jnp.pad(lines, ((0, 0), (0, 0), (0, 0), (0, extra * width - lines.shape[-1])))
    lines = lines.reshape(2, chips, g, extra, width).astype(BF)
    own = lax.axis_index("core")
    line_mine = add_cores(
        lax.dynamic_index_in_dim(lines, own, 0, keepdims=False),
        lax.dynamic_index_in_dim(lines, 1 - own, 0, keepdims=False),
    )
    if (lax.axis_size("z"), lax.axis_size("x"), g) == (4, 2, 2):
        tail = jnp.concatenate([matrix_mine[:, :, 2 * per :], line_mine], axis=2)
        last = [add_chips_stepwise(matrix_mine[:, :, : 2 * per], True), add_chips_stepwise(tail, False)]
        last = jnp.concatenate(last, axis=0)
    else:
        last = add_chips(jnp.concatenate([matrix_mine, line_mine], axis=2))
    dw = [last[m * per : (m + 1) * per] for m in range(3)] + [up_sum[:, -width:]]
    up_sum = up_sum[:, :-width]
    line = last[3 * per :].reshape(extra * width)
    grads = [line[m * small : (m + 1) * small] for m in range(8)]
    gain_one, shift_one, query_add, value_add, output_add, gain_two, shift_two, down_add = grads
    up_add = line[8 * small : 8 * small + wide]
    return (
        output, input_grad, gain_one, shift_one, dw[0], query_add, dw[1], dw[2], value_add, dw[3], output_add,
        gain_two, shift_two, up_sum, up_add, down_sum, down_add,
    )


def solution(mesh):
    dp, g = mesh.shape["dp"], mesh.shape["seq"]
    fine = Mesh(mesh.devices.reshape(4, dp // 8, 2, g), ("z", "x", "core", "seq"))
    both = ("z", "x", "core")
    rows, vector, matrix = P(both, "seq", None), P(both + ("seq",)), P(both, "seq")
    in_specs = (
        rows, vector, vector, matrix, vector, matrix, matrix, vector, matrix, vector, vector, vector, matrix,
        vector, matrix, vector, P(both, None), rows,
    )
    out_specs = (
        rows, rows, vector, vector, matrix, vector, matrix, matrix, vector, matrix, vector, vector, vector,
        matrix, vector, matrix, vector,
    )
    return jax.shard_map(body, mesh=fine, in_specs=in_specs, out_specs=out_specs, check_vma=False)
```

```python
import functools
import itertools
import math

import jax
import jax.numpy as jnp
from jax import lax
from jax.experimental import pallas as pl
from jax.experimental.pallas import tpu as pltpu
from jax.sharding import Mesh, PartitionSpec as P

HEAD_DIM = 64
PIECE = 256
NEGATIVE = -1e30
EPSILON = 1e-05
BENDING = math.sqrt(2.0 / math.pi)
CUBIC_TERM = 0.044715
SCALE = HEAD_DIM**-0.5
LOG2E = math.log2(math.e)

BF = jnp.bfloat16
F32 = jnp.float32
VMEM_LIMIT = 60 * 2**20
COST_PARTS = 1

NN = (((1,), (0,)), ((), ()))
NT = (((1,), (1,)), ((), ()))
TN = (((0,), (0,)), ((), ()))


def dot(left, right, form):
    return lax.dot_general(left, right, form, preferred_element_type=F32)


def params():
    return pltpu.CompilerParams(vmem_limit_bytes=VMEM_LIMIT)


def cost(flops, nbytes, trans=0):
    part = lambda n: int(n) // COST_PARTS
    return pl.CostEstimate(flops=part(flops), bytes_accessed=part(nbytes), transcendentals=part(trans))


def shape(dims, dtype):
    return jax.ShapeDtypeStruct(dims, dtype)


def once(block, index):
    return pl.BlockSpec(block, index, pipeline_mode=pl.Buffered(1))


def after(values, *earlier):
    return lax.optimization_barrier((values,) + earlier)[0]


def norm_parts(values):
    centre = values - jnp.mean(values, axis=-1, keepdims=True)
    inverse = lax.rsqrt(jnp.mean(centre * centre, axis=-1, keepdims=True) + EPSILON)
    return centre * inverse, inverse


def norm_back(upstream, hat, inverse, gain):
    scaled = upstream * gain
    return inverse * (
        scaled
        - jnp.mean(scaled, axis=-1, keepdims=True)
        - hat * jnp.mean(scaled * hat, axis=-1, keepdims=True)
    )


def fold(values):
    rows, columns = values.shape
    return jnp.sum(values.reshape(rows // 8, 8, columns), axis=0)


def clear_at_start(*refs):
    @pl.when(pl.program_id(0) == 0)
    def _():
        for ref in refs:
            ref[...] = jnp.zeros_like(ref)


GAIN_ONE, SHIFT_ONE, QUERY_BIAS, VALUE_BIAS, OUTPUT_BIAS, GAIN_TWO, SHIFT_TWO, DOWN_BIAS = range(8)


def row(ref, index):
    return ref[index : index + 1, :]


def weight_columns(ref, j, rows=slice(None)):
    block = ref[:, j, rows, :]
    return block.reshape(block.shape[0] * block.shape[1], block.shape[2])


def pack_body(*refs):
    out = refs[-1]
    out[...] = jnp.zeros_like(out)
    at = 0
    for ref in refs[:-1]:
        out[at : at + ref.shape[0], : ref.shape[1]] = ref[...]
        at += ref.shape[0]


def pack(matrices, vectors, extra):
    rows = sum(m.shape[0] for m in matrices) + extra
    return pl.pallas_call(
        pack_body,
        out_shape=shape((rows, matrices[0].shape[1]), BF),
        compiler_params=params(),
        name="pack",
    )(*matrices, *[v.reshape(1, -1) for v in vectors])


def project_body(x_ref, vec_ref, w_ref, x1_ref, q_ref, k_ref, v_ref):
    hat, _ = norm_parts(x_ref[...].astype(F32))
    x1 = (hat * row(vec_ref, GAIN_ONE) + row(vec_ref, SHIFT_ONE)).astype(BF)
    x1_ref[...] = x1
    groups, per, width = w_ref.shape[1], w_ref.shape[2] // 3, w_ref.shape[3]
    for m, (out, bias) in enumerate(((q_ref, QUERY_BIAS), (k_ref, None), (v_ref, VALUE_BIAS))):
        for j in range(groups):
            at = slice(j * width, (j + 1) * width)
            y = dot(x1, weight_columns(w_ref, j, slice(m * per, (m + 1) * per)), NN)
            if bias is not None:
                y = y + vec_ref[bias : bias + 1, at]
            out[:, at] = y.astype(BF)


def project(x, vec, first, tile):
    tokens, d = x.shape
    dp, g, rows, width = first.shape
    per = d // dp
    tok = pl.BlockSpec((tile, d), lambda i: (i, 0))
    return pl.pallas_call(
        project_body,
        grid=(tokens // tile,),
        in_specs=[tok, once((8, d), lambda i: (0, 0)), once((dp, g, 3 * per, width), lambda i: (0, 0, 0, 0))],
        out_specs=[tok] * 4,
        out_shape=[shape((tokens, d), BF)] * 4,
        compiler_params=params(),
        cost_estimate=cost(6 * tokens * d * d, 10 * tokens * d + 6 * d * d),
        name="project",
    )(x, vec, first)


def reach_of(places, first, second):
    in_first = (places >= first) & (places < first + PIECE)
    in_second = (places >= second) & (places < second + PIECE)
    return jnp.where(in_first, first + (PIECE - 1), jnp.where(in_second, second + (PIECE - 1), places))


def query_groups(starts_ref, offset_ref, queries, keys, fixed_offset, per, run):
    b = pl.program_id(0)
    first, second = starts_ref[b, 0], starts_ref[b, 1]
    offset = offset_ref[0]
    block = min(256, queries)
    count = queries // block

    def options(n):
        return range(n + 1, min(n + 2, keys // 256) + 1) if fixed_offset else range(1, keys // 256 + 1)

    def item(n, tiles):
        places = offset + n * block + lax.broadcasted_iota(jnp.int32, (1, block), 1)
        clear = n * 256 if fixed_offset else 0
        return slice(n * block, (n + 1) * block), clear, tiles * 256, reach_of(places, first, second)

    last = [reach_of(offset + (n + 1) * block - 1, first, second) for n in range(count)]
    for begin in range(0, count, per):
        group = range(begin, min(begin + per, count))
        for tiles in itertools.product(*[options(n) for n in group]):
            fits = [(last[n] >= (t - 1) * 256) & (last[n] < t * 256) for n, t in zip(group, tiles)]

            @pl.when(functools.reduce(jnp.logical_and, fits))
            def _(group=group, tiles=tiles):
                run([item(n, t) for n, t in zip(group, tiles)])


def hide(scores, clear, reach):
    span, block = scores.shape
    places = clear + lax.broadcasted_iota(jnp.int32, (span - clear, block), 0)
    tail = jnp.where(places <= reach, scores[clear:], NEGATIVE)
    return tail if clear == 0 else jnp.concatenate([scores[:clear], tail], axis=0)


def head_masks():
    lanes = lax.broadcasted_iota(jnp.int32, (1, 2 * HEAD_DIM), 1)
    return [lanes < HEAD_DIM, lanes >= HEAD_DIM]


def pick(mask, values):
    return jnp.where(mask, values, jnp.zeros_like(values))


def staggered(count, ahead, start, finish):
    for i in range(min(ahead, count)):
        start(i)
    for i in range(count):
        if i + ahead < count:
            start(i + ahead)
        finish(i)


POWER = SCALE * LOG2E
SAFE = 2.0**100


def attend_body(fixed_offset, starts_ref, offset_ref, q_ref, k_ref, v_ref, out_ref, lse_ref, vt_ref, worst_ref):
    masks = head_masks()
    queries, keys = q_ref.shape[1], k_ref.shape[1]
    pairs = q_ref.shape[2] // 128
    for p in range(pairs):
        vt_ref[p * 128 : (p + 1) * 128, :] = v_ref[0, :, p * 128 : (p + 1) * 128].T
    worst_ref[...] = jnp.zeros_like(worst_ref)

    def run(exact, items):
        units = [(it, p, h) for it in items for p in range(pairs) for h in range(2)]
        held = [None] * len(units)

        def start(i):
            (at, clear, span, reach), p, h = units[i]
            lanes = slice(p * 128, (p + 1) * 128)
            held[i] = hide(dot(k_ref[0, :span, lanes], pick(masks[h], q_ref[0, at, lanes]), NT), clear, reach)

        def finish(i):
            (at, _, span, _), p, h = units[i]
            s = held[i]
            top = jnp.max(s, axis=0, keepdims=True) if exact else s[:1]
            raised = jnp.exp2((s - top) * POWER)
            size = jnp.sum(raised, axis=0, keepdims=True)
            if not exact:
                worst_ref[...] = jnp.maximum(worst_ref[...], size)
            lse_ref[0, p, h : h + 1, at] = top * POWER + jnp.log2(size)
            mine = slice(p * 128 + h * HEAD_DIM, p * 128 + (h + 1) * HEAD_DIM)
            total = dot(vt_ref[mine, :span], raised.astype(BF), NN)
            out_ref[mine, at] = (total * (1.0 / size)).astype(BF)

        staggered(len(units), 2, start, finish)

    args = (starts_ref, offset_ref, queries, keys, fixed_offset)
    query_groups(*args, 2, functools.partial(run, False))

    @pl.when(jnp.max(worst_ref[...]) >= SAFE)
    def _():
        query_groups(*args, 1, functools.partial(run, True))


def attend(starts, offset, q, k, v, fixed_offset):
    count, queries, d = q.shape
    keys = k.shape[1]
    lanes = 256
    rows = lambda n: pl.BlockSpec((1, n, lanes), lambda b, p, *_: (b, 0, p))
    return pl.pallas_call(
        functools.partial(attend_body, fixed_offset),
        grid_spec=pltpu.PrefetchScalarGridSpec(
            num_scalar_prefetch=2,
            grid=(count, d // lanes),
            in_specs=[rows(queries), rows(keys), rows(keys)],
            out_specs=[
                pl.BlockSpec((lanes, queries), lambda b, p, *_: (p, b)),
                pl.BlockSpec((1, lanes // 128, 2, queries), lambda b, p, *_: (b, p, 0, 0)),
            ],
            scratch_shapes=[pltpu.VMEM((lanes, keys), BF), pltpu.VMEM((1, min(256, queries)), F32)],
        ),
        out_shape=[shape((d, count * queries), BF), shape((count, d // 128, 2, queries), F32)],
        compiler_params=params(),
        cost_estimate=cost(12 * count * queries * keys * d, 8 * count * keys * d, count * d // 64 * queries * keys),
        name="attend",
    )(starts, offset, q, k, v)


def attend_back_body(
    fixed_offset, starts_ref, offset_ref, q_ref, k_ref, v_ref, g_ref, att_ref, lse_ref,
    dq_ref, dkv_ref, kt_ref, settled_ref, dk_acc, dv_acc,
):
    masks = head_masks()
    queries, keys = q_ref.shape[1], k_ref.shape[1]
    pairs = q_ref.shape[2] // 128
    dk_acc[...] = jnp.zeros_like(dk_acc)
    dv_acc[...] = jnp.zeros_like(dv_acc)
    for p in range(pairs):
        lanes = slice(p * 128, (p + 1) * 128)
        kt_ref[lanes, :] = k_ref[0, :, lanes].T
        both = g_ref[0, :, lanes].T.astype(F32) * att_ref[lanes, :].astype(F32)
        for h in range(2):
            part = both[h * HEAD_DIM : (h + 1) * HEAD_DIM]
            settled_ref[2 * p + h : 2 * p + h + 1, :] = jnp.sum(part, axis=0, keepdims=True)

    def run(items):
        units = [(it, p, h) for it in items for p in range(pairs) for h in range(2)]
        held = [None] * len(units)
        done = {}

        def start(i):
            (at, clear, span, reach), p, h = units[i]
            lanes = slice(p * 128, (p + 1) * 128)
            q, g = pick(masks[h], q_ref[0, at, lanes]), pick(masks[h], g_ref[0, at, lanes])
            s = hide(dot(k_ref[0, :span, lanes], q, NT), clear, reach)
            held[i] = (s, dot(v_ref[0, :span, lanes], g, NT), q, g)

        def finish(i):
            (at, _, span, _), p, h = units[i]
            s, chance_grad, q, g = held[i]
            n = 2 * p + h
            chances = jnp.exp2(s * POWER - lse_ref[0, p, h : h + 1, at])
            ds = (chances * (chance_grad - settled_ref[n : n + 1, at])).astype(BF)
            dq = dot(kt_ref[n * HEAD_DIM : (n + 1) * HEAD_DIM, :span], ds, NN)
            done[h] = (chances.astype(BF), ds, q, g, dq)
            if h == 1:
                lanes = slice(p * 128, (p + 1) * 128)
                join = lambda m, axis: jnp.concatenate([done[0][m], done[1][m]], axis=axis)
                dv_acc[:span, lanes] += dot(join(0, 1), join(3, 0), NN)
                dk_acc[:span, lanes] += dot(join(1, 1), join(2, 0), NN)
                dq_ref[0, at, lanes] = (join(4, 0).T * SCALE).astype(BF)

        staggered(len(units), 2, start, finish)

    query_groups(starts_ref, offset_ref, queries, keys, fixed_offset, 2, run)
    dkv_ref[0, 0] = (dk_acc[...] * SCALE).astype(BF)
    dkv_ref[1, 0] = dv_acc[...].astype(BF)


def attend_back(starts, offset, q, k, v, g, att, lse, fixed_offset):
    count, queries, d = q.shape
    keys = k.shape[1]
    lanes = 256
    rows = lambda n: pl.BlockSpec((1, n, lanes), lambda b, p, *_: (b, 0, p))
    return pl.pallas_call(
        functools.partial(attend_back_body, fixed_offset),
        grid_spec=pltpu.PrefetchScalarGridSpec(
            num_scalar_prefetch=2,
            grid=(count, d // lanes),
            in_specs=[
                rows(queries),
                rows(keys),
                rows(keys),
                rows(queries),
                pl.BlockSpec((lanes, queries), lambda b, p, *_: (p, b)),
                pl.BlockSpec((1, lanes // 128, 2, queries), lambda b, p, *_: (b, p, 0, 0)),
            ],
            out_specs=[
                rows(queries),
                pl.BlockSpec((2, 1, keys, lanes), lambda b, p, *_: (0, b, 0, p)),
            ],
            scratch_shapes=[
                pltpu.VMEM((lanes, keys), BF),
                pltpu.VMEM((lanes // HEAD_DIM, queries), F32),
                pltpu.VMEM((keys, lanes), F32),
                pltpu.VMEM((keys, lanes), F32),
            ],
        ),
        out_shape=[shape((count, queries, d), BF), shape((2, count, keys, d), BF)],
        compiler_params=params(),
        cost_estimate=cost(30 * count * queries * keys * d, 14 * count * keys * d, count * d // 64 * queries * keys),
        name="attend_back",
    )(starts, offset, q, k, v, g, att, lse)


def hidden_chunk(up_ref):
    return min(512, up_ref.shape[3])


def up_chunk(up_ref, n, size):
    per = up_ref.shape[3] // size
    block = up_ref[:, n // per, :, (n % per) * size : (n % per + 1) * size]
    return block.reshape(block.shape[0] * block.shape[1], size)


def rise_body(x_ref, att_ref, vec_ref, upb_ref, wo_ref, up_ref, mid_ref, x2_ref, act_ref, slope_ref):
    att = att_ref[...]
    width = wo_ref.shape[3]
    parts = [dot(att, weight_columns(wo_ref, j), TN) for j in range(wo_ref.shape[1])]
    branch = jnp.concatenate(parts, axis=1)
    middle = x_ref[...].astype(F32) + (branch + row(vec_ref, OUTPUT_BIAS))
    mid_ref[...] = middle
    hat, _ = norm_parts(middle)
    x2 = (hat * row(vec_ref, GAIN_TWO) + row(vec_ref, SHIFT_TWO)).astype(BF)
    x2_ref[...] = x2
    size = hidden_chunk(up_ref)
    for n in range(up_ref.shape[1] * up_ref.shape[3] // size):
        at = slice(n * size, (n + 1) * size)
        x = dot(x2, up_chunk(up_ref, n, size), NN) + upb_ref[:, at]
        square = x * x
        t = jnp.tanh(x * (BENDING + (BENDING * CUBIC_TERM) * square))
        half = 0.5 * (1.0 + t)
        act_ref[:, at] = (x * half).astype(BF)
        bend = (0.5 * BENDING) * x * (1.0 + (3.0 * CUBIC_TERM) * square)
        slope_ref[:, at] = (half + bend * (1.0 - t * t)).astype(BF)


def rise(x, att, vec, upb, first, up, tile):
    tokens, d = x.shape
    dp, g, _, width = first.shape
    per = d // dp
    ff = upb.shape[1]
    tok = pl.BlockSpec((tile, d), lambda i: (i, 0))
    wide = pl.BlockSpec((tile, ff), lambda i: (i, 0))
    return pl.pallas_call(
        rise_body,
        grid=(tokens // tile,),
        in_specs=[
            tok,
            pl.BlockSpec((d, tile), lambda i: (0, i)),
            once((8, d), lambda i: (0, 0)),
            once((1, ff), lambda i: (0, 0)),
            once((dp, g, per, width), lambda i: (0, 0, 3, 0)),
            once(up.shape, lambda i: (0, 0, 0, 0)),
        ],
        out_specs=[tok, tok, wide, wide],
        out_shape=[shape((tokens, d), F32), shape((tokens, d), BF), shape((tokens, ff), BF), shape((tokens, ff), BF)],
        compiler_params=params(),
        cost_estimate=cost(2 * tokens * d * (d + ff), tokens * (10 * d + 4 * ff) + 2 * d * (d + ff), tokens * ff),
        name="rise",
    )(x, att, vec, upb, first, up)


def fall_body(
    begun, which_ref, mid_ref, act_ref, slope_ref, og_ref, vec_ref, wo_ref, up_ref, down_ref, *rest
):
    out_ref, bg_ref, mg_ref, br_ref, dat_ref, upb_ref, sums_ref = rest[4:] if begun else rest
    clear_at_start(upb_ref, sums_ref)
    og = og_ref[...]
    incoming = og.astype(F32)
    g, width = down_ref.shape[1], down_ref.shape[3]
    size = hidden_chunk(up_ref)
    per = size // down_ref.shape[2]
    chunks = up_ref.shape[1] * up_ref.shape[3] // size
    outs = [None] * g
    e = None
    for n in range(chunks):
        at = slice(n * size, (n + 1) * size)
        act = act_ref[:, at]
        rise_grad = None
        for j in range(g):
            block = down_ref[n * per : (n + 1) * per, j].reshape(size, width)
            part = dot(og[:, j * width : (j + 1) * width], block, NT)
            rise_grad = part if rise_grad is None else rise_grad + part
            part = dot(act, block, NN)
            outs[j] = part if outs[j] is None else outs[j] + part
        bg = (slope_ref[:, at].astype(F32) * rise_grad).astype(BF)
        bg_ref[:, at] = bg
        upb_ref[:, at] += fold(bg.astype(F32))
        part = dot(bg, up_chunk(up_ref, n, size), NT)
        e = part if e is None else e + part
    middle = mid_ref[...]
    out_ref[...] = (middle + (jnp.concatenate(outs, axis=1) + row(vec_ref, DOWN_BIAS))).astype(BF)
    hat, inverse = norm_parts(middle)
    middle_grad = incoming + norm_back(e, hat, inverse, row(vec_ref, GAIN_TWO))
    mg_ref[...] = middle_grad
    branch = middle_grad.astype(BF)
    br_ref[...] = branch
    back = None
    for j in range(wo_ref.shape[1]):
        part = dot(branch[:, j * width : (j + 1) * width], weight_columns(wo_ref, j), NT)
        back = part if back is None else back + part
    dat_ref[...] = back.astype(BF)
    sums_ref[0] += fold(e * hat)
    sums_ref[1] += fold(e)
    sums_ref[2] += fold(branch.astype(F32))
    sums_ref[3] += fold(incoming)


def fall(middle, act, slope, og, vec, first, up, down, tile, which, sequences, halves, begun=()):
    tokens, d = og.shape
    dp, g, _, width = first.shape
    per = d // dp
    ff = act.shape[1]
    per_half = tokens // tile // sequences // halves
    kept = tokens // halves

    def block(i, w):
        return (i // per_half) * (per_half * halves) + w[0] * per_half + i % per_half, 0

    tok = pl.BlockSpec((tile, d), block)
    wide = pl.BlockSpec((tile, ff), block)
    fixed = lambda dims: once(dims, lambda i, w: (0,) * len(dims))
    return pl.pallas_call(
        functools.partial(fall_body, bool(begun)),
        grid_spec=pltpu.PrefetchScalarGridSpec(
            num_scalar_prefetch=1,
            grid=(kept // tile,),
            in_specs=[
                tok, wide, wide, tok,
                fixed((8, d)),
                once((dp, g, per, width), lambda i, w: (0, 0, 3, 0)),
                fixed(up.shape),
                fixed(down.shape),
            ] + [pl.BlockSpec(memory_space=pl.ANY)] * len(begun),
            out_specs=[
                pl.BlockSpec((tile, d), lambda i, w: (i, 0)), wide, tok, tok, tok,
                pl.BlockSpec((8, ff), lambda i, w: (0, 0)),
                pl.BlockSpec((4, 8, d), lambda i, w: (0, 0, 0)),
            ],
        ),
        out_shape=[
            shape((kept, d), BF), shape((tokens, ff), BF), shape((tokens, d), F32), shape((tokens, d), BF),
            shape((tokens, d), BF), shape((8, ff), F32), shape((4, 8, d), F32),
        ],
        input_output_aliases={9 + n: 1 + n for n in range(len(begun))},
        compiler_params=params(),
        cost_estimate=cost(2 * kept * d * (d + 3 * ff), kept * (16 * d + 6 * ff) + 2 * d * (d + 2 * ff)),
        name="fall",
    )(which, middle, act, slope, og, vec, first, up, down, *begun)


def split_cores(core_ref, values, keep_ref, send_ref):
    even, odd = values[:, 0], values[:, 1]
    mine = core_ref[0] == 0
    keep_ref[...] = jnp.where(mine, even, odd).astype(BF)
    send_ref[...] = jnp.where(mine, odd, even).astype(BF)


def down_grad_body(core_ref, act_ref, og_ref, keep_ref, send_ref):
    y = dot(act_ref[...], og_ref[...], TN)
    chips, g, rows, width = keep_ref.shape
    for j in range(g):
        part = y[:, j * width : (j + 1) * width].reshape(chips, 2, rows, width)
        split_cores(core_ref, part, keep_ref.at[:, j], send_ref.at[:, j])


def down_grad(core, act, og, dp, g):
    tokens, ff = act.shape
    d = og.shape[1]
    size = min(512, ff)
    rows, width = ff // dp, d // g
    chips = size // rows // 2
    out = pl.BlockSpec((chips, g, rows, width), lambda i, *_: (i, 0, 0, 0))
    return pl.pallas_call(
        down_grad_body,
        grid_spec=pltpu.PrefetchScalarGridSpec(
            num_scalar_prefetch=1,
            grid=(ff // size,),
            in_specs=[pl.BlockSpec((tokens, size), lambda i, *_: (0, i)), once((tokens, d), lambda i, *_: (0, 0))],
            out_specs=[out, out],
        ),
        out_shape=[shape((dp // 2, g, rows, width), BF)] * 2,
        compiler_params=params(),
        cost_estimate=cost(2 * tokens * d * ff, 2 * (tokens * (d + ff) + d * ff)),
        name="down_grad",
    )(core, act, og)


def weight_grad_body(form, core_ref, x_ref, dy_ref, keep_ref, send_ref):
    dy = dy_ref[...]
    y = dot(x_ref[...], dy.reshape(dy.shape[-2:]), form)
    chips, _, rows, width = keep_ref.shape
    split_cores(core_ref, y.reshape(chips, 2, rows, width), keep_ref.at[:, 0], send_ref.at[:, 0])


def weight_grad(core, x, dy, dp, g, form, name):
    count, tokens, columns = dy.shape
    d = x.shape[0] if form == NN else x.shape[1]
    share = columns // g
    size = min(512, share)
    per = share // size
    rows = d // dp
    out = pl.BlockSpec((dp // 2, 1, rows, size), lambda m, i, *_: (0, i // per, m, i % per))
    return pl.pallas_call(
        functools.partial(weight_grad_body, form),
        grid_spec=pltpu.PrefetchScalarGridSpec(
            num_scalar_prefetch=1,
            grid=(count, columns // size),
            in_specs=[
                once(x.shape, lambda m, i, *_: (0, 0)),
                pl.BlockSpec((1, tokens, size), lambda m, i, *_: (m, 0, i)),
            ],
            out_specs=[out, out],
        ),
        out_shape=[shape((dp // 2, g, count * rows, share), BF)] * 2,
        compiler_params=params(),
        cost_estimate=cost(2 * count * tokens * d * columns, 2 * (tokens * d + count * columns * (tokens + d))),
        name=name,
    )(core, x, dy)


def input_body(which_ref, x_ref, mg_ref, dq_ref, dkv_ref, vec_ref, w_ref, out_ref, sums_ref):
    clear_at_start(sums_ref)
    groups, per, width = w_ref.shape[1], w_ref.shape[2] // 3, w_ref.shape[3]
    e = None
    grads = (dq_ref[...], dkv_ref[0], dkv_ref[1])
    for m in range(3):
        for j in range(groups):
            at = slice(j * width, (j + 1) * width)
            part = dot(grads[m][:, at], weight_columns(w_ref, j, slice(m * per, (m + 1) * per)), NT)
            e = part if e is None else e + part
    hat, inverse = norm_parts(x_ref[...].astype(F32))
    out_ref[...] = (mg_ref[...] + norm_back(e, hat, inverse, row(vec_ref, GAIN_ONE))).astype(BF)
    sums_ref[0] += fold(e * hat)
    sums_ref[1] += fold(e)
    sums_ref[2] += fold(grads[0].astype(F32))
    sums_ref[3] += fold(grads[2].astype(F32))


def input_back(x, mg, dq, dkv, vec, first, tile, which, sequences, halves):
    tokens, d = x.shape
    dp, g, rows, width = first.shape
    per = d // dp
    per_half = tokens // tile // sequences // halves

    def block(i, which):
        return (i // per_half) * (per_half * halves) + which[0] * per_half + i % per_half

    tok = pl.BlockSpec((tile, d), lambda i, w: (block(i, w), 0))
    kept = tokens // halves
    return pl.pallas_call(
        input_body,
        grid_spec=pltpu.PrefetchScalarGridSpec(
            num_scalar_prefetch=1,
            grid=(kept // tile,),
            in_specs=[
                tok, tok, tok,
                pl.BlockSpec((2, tile, d), lambda i, w: (0, block(i, w), 0)),
                once((8, d), lambda i, w: (0, 0)),
                once((dp, g, 3 * per, width), lambda i, w: (0, 0, 0, 0)),
            ],
            out_specs=[
                pl.BlockSpec((tile, d), lambda i, w: (i, 0)),
                pl.BlockSpec((4, 8, d), lambda i, w: (0, 0, 0)),
            ],
        ),
        out_shape=[shape((kept, d), BF), shape((4, 8, d), F32)],
        compiler_params=params(),
        cost_estimate=cost(6 * kept * d * d, 16 * kept * d + 6 * d * d),
        name="input_back",
    )(which, x, mg, dq, dkv, vec, first)


def swap_cores(values):
    return lax.ppermute(values, "core", [(0, 1), (1, 0)])


def add_cores(keep, send):
    return (keep.astype(F32) + swap_cores(send).astype(F32)).astype(BF)


def add_chips(mine):
    chips, g = mine.shape[:2]
    flat = mine.reshape((chips * g,) + mine.shape[2:])
    return lax.psum_scatter(flat, ("z", "x", "seq"), scatter_dimension=0, tiled=True)[0].astype(F32)


NEAR = ("z", [(0, 1), (1, 0), (2, 3), (3, 2)])
FAR = ("z", [(0, 2), (2, 0), (1, 3), (3, 1)])
ACROSS = ("x", [(0, 1), (1, 0)])
ALONG = ("seq", [(0, 1), (1, 0)])


def cut(values, dim, own, route):
    keep = lax.dynamic_index_in_dim(values, own, dim, keepdims=False)
    return keep, lax.dynamic_index_in_dim(values, 1 - own, dim, keepdims=False), route


def add_step(step, came):
    return (step[0].astype(F32) + came.astype(F32)).astype(BF)


def halve(values, dim, own, route):
    step = cut(values, dim, own, route)
    return add_step(step, lax.ppermute(step[1], *route))


def start_step(mine, across_first):
    values = mine.reshape((2, 2, 2) + mine.shape[1:])
    if across_first:
        return cut(values, 2, lax.axis_index("x"), ACROSS)
    return cut(values, 1, lax.axis_index("z") % 2, NEAR)


def next_step(values, across_first):
    if across_first:
        return cut(values, 1, lax.axis_index("z") % 2, NEAR)
    return cut(values, 0, lax.axis_index("z") // 2, FAR)


def last_steps(values, across_first):
    if across_first:
        values = halve(values, 0, lax.axis_index("z") // 2, FAR)
    else:
        values = halve(values, 0, lax.axis_index("x"), ACROSS)
    return halve(values, 0, lax.axis_index("seq"), ALONG).astype(F32)


def all_steps(mine):
    step = start_step(mine, True)
    step = next_step(add_step(step, lax.ppermute(step[1], *step[2])), True)
    return last_steps(add_step(step, lax.ppermute(step[1], *step[2])), True)


def body(
    tokens, first_gain, first_shift, query_weight, query_bias, key_weight, value_weight, value_bias,
    output_weight, output_bias, second_gain, second_shift, up_weight, up_bias, down_weight, down_bias,
    piece_starts, out_grad,
):
    chips, g = lax.axis_size("z") * lax.axis_size("x"), lax.axis_size("seq")
    dp = 2 * chips
    everyone = ("z", "x", "core", "seq")
    count, local, d = tokens.shape
    width = query_weight.shape[1]
    per = query_weight.shape[0]
    small = first_gain.shape[0]
    wide = up_bias.shape[0]
    ff = wide * dp * g
    length = local * g
    place = lax.axis_index("seq")
    core = lax.axis_index("core").astype(jnp.int32).reshape(1)
    paired = g == 2 and count % 2 == 0

    vectors = [first_gain, first_shift, query_bias, value_bias, output_bias, second_gain, second_shift, down_bias]
    extra = 16
    packed = pack([query_weight, key_weight, value_weight, output_weight], vectors + [up_bias], extra)
    first = lax.all_gather(packed, everyone, axis=0).reshape(dp, g, 4 * per + extra, width)
    up = lax.all_gather(up_weight, everyone, axis=0).reshape((dp, g) + up_weight.shape)
    down = lax.all_gather(down_weight, everyone, axis=0).reshape((dp, g) + down_weight.shape)

    if paired:
        half = count // 2

        def swap_rows(values, *earlier):
            sent = lax.dynamic_slice_in_dim(values, (1 - place) * half, half, 0)
            return lax.ppermute(after(sent, *earlier), "seq", [(0, 1), (1, 0)])

        def gather_rows(values, came):
            kept = lax.dynamic_slice_in_dim(values, place * half, half, 0)
            low = jnp.where(place == 0, kept, came)
            high = jnp.where(place == 0, came, kept)
            return jnp.concatenate([low, high], axis=1).reshape(half * length, d)

        def join_rows(kept, came):
            low = jnp.where(place == 0, kept, came)
            high = jnp.where(place == 0, came, kept)
            return jnp.concatenate([low, high], axis=0)

        starts = lax.dynamic_slice_in_dim(piece_starts, place * half, half, 0)
        offset = jnp.zeros((1,), jnp.int32)
        sequences, queries = half, length
    else:
        swap_rows = lambda values, *earlier: values
        gather_rows = lambda values, came: values.reshape(count * local, d)
        starts = piece_starts
        offset = (place * local).astype(jnp.int32).reshape(1)
        sequences, queries = count, local

    rows = sequences * queries
    tile = min(256, rows)
    x = gather_rows(tokens, swap_rows(tokens))
    first = after(first, x)
    vec = first[:, :, 4 * per : 4 * per + 8, :small].astype(F32).transpose(2, 0, 1, 3).reshape(8, d)
    upb = first[:, :, 4 * per + 8, :wide].astype(F32).reshape(1, ff)
    came = swap_rows(out_grad, first)
    x1, q, k, v = project(x, vec, first, tile)
    q, k, v = (t.reshape(sequences, queries, d) for t in (q, k, v))
    if not paired:
        k, v = (lax.all_gather(t, "seq", axis=1, tiled=True) for t in (k, v))
    att, lse = attend(starts, offset, q, k, v, paired)
    og = gather_rows(out_grad, after(came, att))
    middle, x2, act, slope = rise(x, att, vec, upb, first, up, tile)
    down_mine = add_cores(*down_grad(core, act, og, dp, g))
    down_sum = add_chips(down_mine)
    act = after(act, down_mine)
    args = (middle, act, slope, og, vec, first, up, down, tile)
    if paired:
        turn = place.astype(jnp.int32).reshape(1)
        out_sent, *begun, upb_sent, two_sent = fall(*args, 1 - turn, sequences, 2)
        out, *begun, upb_sums, sums_two = fall(*args, turn, sequences, 2, tuple(begun))
        bg, mg, branch, dat = begun
        upb_sums, sums_two = upb_sums + upb_sent, sums_two + two_sent
        came_out = lax.ppermute(out_sent.reshape(half, local, d), *ALONG)
    else:
        out, bg, mg, branch, dat, upb_sums, sums_two = fall(*args, jnp.zeros((1,), jnp.int32), sequences, 1)
        output = out.reshape(count, local, d)
    up_parts = weight_grad(core, x2, bg[None], dp, g, TN, "up_grad")
    out_parts = weight_grad(core, att, branch[None], dp, g, NN, "out_grad")
    if paired:
        up_parts, out_parts, came_out = lax.optimization_barrier((up_parts, out_parts, came_out))
        output = join_rows(out.reshape(half, local, d), came_out)
    up_mine = jnp.concatenate([add_cores(*up_parts), add_cores(*out_parts)], axis=-1)
    up_sum = add_chips(up_mine)
    dat = after(dat, up_mine, down_sum)
    dq, dkv = attend_back(starts, offset, q, k, v, dat.reshape(sequences, queries, d), att, lse, paired)
    dq = dq.reshape(rows, d)
    if not paired:
        dkv = lax.psum_scatter(dkv, "seq", scatter_dimension=2, tiled=True)
    dkv = dkv.reshape(2, rows, d)
    query_parts = weight_grad(core, x1, dq[None], dp, g, TN, "query_grad")
    kv_parts = weight_grad(core, x1, dkv, dp, g, TN, "key_value_grad")
    query_mine, kv_mine = add_cores(*query_parts), add_cores(*kv_parts)
    first_parts = jnp.concatenate([query_mine, kv_mine[:, :, :per]], axis=2)
    second_parts = kv_mine[:, :, per:]
    stepwise = (lax.axis_size("z"), lax.axis_size("x"), g) == (4, 2, 2)
    dkv = after(dkv, first_parts, second_parts, up_sum)
    args = (x, mg, dq, dkv, vec, first, tile)
    if paired:
        sent, sums_sent = input_back(*args, 1 - turn, sequences, 2)
        came_in = lax.ppermute(sent.reshape(half, local, d), *ALONG)
        if stepwise:
            steps = [start_step(first_parts, True), start_step(second_parts, False)]
            arrived = [after(lax.ppermute(move, *route), sent) for _, move, route in steps]
            steps = [next_step(add_step(step, move), n == 0) for n, (step, move) in enumerate(zip(steps, arrived))]
            arrived = [lax.ppermute(move, *route) for _, move, route in steps]
            args = args[:3] + (after(dkv, steps[0][1], steps[1][1]),) + args[4:]
        in_grad, sums_one = input_back(*args, turn, sequences, 2)
        if stepwise:
            arrived[0], arrived[1], came_in, sums_one = lax.optimization_barrier((*arrived, came_in, sums_one))
            summed = [add_step(step, move) for step, move in zip(steps, arrived)]
        sums_one = sums_one + sums_sent
        came_in = lax.ppermute(sent.reshape(half, local, d), "seq", [(0, 1), (1, 0)])
        input_grad = join_rows(in_grad.reshape(half, local, d), came_in)
    else:
        in_grad, sums_one = input_back(*args, jnp.zeros((1,), jnp.int32), sequences, 1)
        input_grad = in_grad.reshape(count, local, d)

    one, two = jnp.sum(sums_one, axis=1), jnp.sum(sums_two, axis=1)
    eight = jnp.stack([one[0], one[1], one[2], one[3], two[2], two[0], two[1], two[3]])
    eight = eight.reshape(8, chips, 2, g, small).transpose(2, 1, 3, 0, 4).reshape(2, chips, g, 8 * small)
    upb_grad = jnp.sum(upb_sums, axis=0).reshape(chips, 2, g, wide).transpose(1, 0, 2, 3)
    lines = jnp.concatenate([eight, upb_grad], axis=-1)
    lines = jnp.pad(lines, ((0, 0), (0, 0), (0, 0), (0, extra * width - lines.shape[-1])))
    lines = lines.reshape(2, chips, g, extra, width).astype(BF)
    own = lax.axis_index("core")
    line_mine = add_cores(
        lax.dynamic_index_in_dim(lines, own, 0, keepdims=False),
        lax.dynamic_index_in_dim(lines, 1 - own, 0, keepdims=False),
    )
    if stepwise:
        last = [last_steps(summed[0], True), last_steps(summed[1], False), all_steps(line_mine)]
        last = jnp.concatenate(last, axis=0)
    else:
        last = add_chips(jnp.concatenate([first_parts, second_parts, line_mine], axis=2))
    dw = [last[m * per : (m + 1) * per] for m in range(3)] + [up_sum[:, -width:]]
    up_sum = up_sum[:, :-width]
    line = last[3 * per :].reshape(extra * width)
    grads = [line[m * small : (m + 1) * small] for m in range(8)]
    gain_one, shift_one, query_add, value_add, output_add, gain_two, shift_two, down_add = grads
    up_add = line[8 * small : 8 * small + wide]
    return (
        output, input_grad, gain_one, shift_one, dw[0], query_add, dw[1], dw[2], value_add, dw[3], output_add,
        gain_two, shift_two, up_sum, up_add, down_sum, down_add,
    )


def solution(mesh):
    dp, g = mesh.shape["dp"], mesh.shape["seq"]
    fine = Mesh(mesh.devices.reshape(4, dp // 8, 2, g), ("z", "x", "core", "seq"))
    both = ("z", "x", "core")
    rows, vector, matrix = P(both, "seq", None), P(both + ("seq",)), P(both, "seq")
    in_specs = (
        rows, vector, vector, matrix, vector, matrix, matrix, vector, matrix, vector, vector, vector, matrix,
        vector, matrix, vector, P(both, None), rows,
    )
    out_specs = (
        rows, rows, vector, vector, matrix, vector, matrix, matrix, vector, matrix, vector, vector, vector,
        matrix, vector, matrix, vector,
    )
    return jax.shard_map(body, mesh=fine, in_specs=in_specs, out_specs=out_specs, check_vma=False)
```

```python
import functools
import itertools
import math

import jax
import jax.numpy as jnp
from jax import lax
from jax.experimental import pallas as pl
from jax.experimental.pallas import tpu as pltpu
from jax.sharding import Mesh, PartitionSpec as P

HEAD_DIM = 64
PIECE = 256
NEGATIVE = -1e30
EPSILON = 1e-05
BENDING = math.sqrt(2.0 / math.pi)
CUBIC_TERM = 0.044715
SCALE = HEAD_DIM**-0.5
LOG2E = math.log2(math.e)

BF = jnp.bfloat16
F32 = jnp.float32
VMEM_LIMIT = 60 * 2**20
COST_PARTS = 1

NN = (((1,), (0,)), ((), ()))
NT = (((1,), (1,)), ((), ()))
TN = (((0,), (0,)), ((), ()))


def dot(left, right, form):
    return lax.dot_general(left, right, form, preferred_element_type=F32)


def params():
    return pltpu.CompilerParams(vmem_limit_bytes=VMEM_LIMIT)


def cost(flops, nbytes, trans=0):
    part = lambda n: int(n) // COST_PARTS
    return pl.CostEstimate(flops=part(flops), bytes_accessed=part(nbytes), transcendentals=part(trans))


def shape(dims, dtype):
    return jax.ShapeDtypeStruct(dims, dtype)


def once(block, index):
    return pl.BlockSpec(block, index, pipeline_mode=pl.Buffered(1))


def after(values, *earlier):
    return lax.optimization_barrier((values,) + earlier)[0]


def norm_parts(values):
    centre = values - jnp.mean(values, axis=-1, keepdims=True)
    inverse = lax.rsqrt(jnp.mean(centre * centre, axis=-1, keepdims=True) + EPSILON)
    return centre * inverse, inverse


def norm_back(upstream, hat, inverse, gain):
    scaled = upstream * gain
    return inverse * (
        scaled
        - jnp.mean(scaled, axis=-1, keepdims=True)
        - hat * jnp.mean(scaled * hat, axis=-1, keepdims=True)
    )


def fold(values):
    rows, columns = values.shape
    return jnp.sum(values.reshape(rows // 8, 8, columns), axis=0)


def clear_at_start(*refs):
    @pl.when(pl.program_id(0) == 0)
    def _():
        for ref in refs:
            ref[...] = jnp.zeros_like(ref)


GAIN_ONE, SHIFT_ONE, QUERY_BIAS, VALUE_BIAS, OUTPUT_BIAS, GAIN_TWO, SHIFT_TWO, DOWN_BIAS = range(8)


def row(ref, index):
    return ref[index : index + 1, :]


def weight_columns(ref, j, rows=slice(None)):
    block = ref[:, j, rows, :]
    return block.reshape(block.shape[0] * block.shape[1], block.shape[2])


def pack_body(*refs):
    out = refs[-1]
    out[...] = jnp.zeros_like(out)
    at = 0
    for ref in refs[:-1]:
        out[at : at + ref.shape[0], : ref.shape[1]] = ref[...]
        at += ref.shape[0]


def pack(matrices, vectors, extra):
    rows = sum(m.shape[0] for m in matrices) + extra
    return pl.pallas_call(
        pack_body,
        out_shape=shape((rows, matrices[0].shape[1]), BF),
        compiler_params=params(),
        name="pack",
    )(*matrices, *[v.reshape(1, -1) for v in vectors])


def project_body(x_ref, vec_ref, w_ref, x1_ref, q_ref, k_ref, v_ref):
    hat, _ = norm_parts(x_ref[...].astype(F32))
    x1 = (hat * row(vec_ref, GAIN_ONE) + row(vec_ref, SHIFT_ONE)).astype(BF)
    x1_ref[...] = x1
    groups, per, width = w_ref.shape[1], w_ref.shape[2] // 3, w_ref.shape[3]
    for m, (out, bias) in enumerate(((q_ref, QUERY_BIAS), (k_ref, None), (v_ref, VALUE_BIAS))):
        for j in range(groups):
            at = slice(j * width, (j + 1) * width)
            y = dot(x1, weight_columns(w_ref, j, slice(m * per, (m + 1) * per)), NN)
            if bias is not None:
                y = y + vec_ref[bias : bias + 1, at]
            out[:, at] = y.astype(BF)


def project(x, vec, first, tile):
    tokens, d = x.shape
    dp, g, rows, width = first.shape
    per = d // dp
    tok = pl.BlockSpec((tile, d), lambda i: (i, 0))
    return pl.pallas_call(
        project_body,
        grid=(tokens // tile,),
        in_specs=[tok, once((8, d), lambda i: (0, 0)), once((dp, g, 3 * per, width), lambda i: (0, 0, 0, 0))],
        out_specs=[tok] * 4,
        out_shape=[shape((tokens, d), BF)] * 4,
        compiler_params=params(),
        cost_estimate=cost(6 * tokens * d * d, 10 * tokens * d + 6 * d * d),
        name="project",
    )(x, vec, first)


def reach_of(places, first, second):
    in_first = (places >= first) & (places < first + PIECE)
    in_second = (places >= second) & (places < second + PIECE)
    return jnp.where(in_first, first + (PIECE - 1), jnp.where(in_second, second + (PIECE - 1), places))


def query_groups(starts_ref, offset_ref, queries, keys, fixed_offset, per, run):
    b = pl.program_id(0)
    first, second = starts_ref[b, 0], starts_ref[b, 1]
    offset = offset_ref[0]
    block = min(256, queries)
    count = queries // block

    def options(n):
        return range(n + 1, min(n + 2, keys // 256) + 1) if fixed_offset else range(1, keys // 256 + 1)

    def item(n, tiles):
        places = offset + n * block + lax.broadcasted_iota(jnp.int32, (1, block), 1)
        clear = n * 256 if fixed_offset else 0
        return slice(n * block, (n + 1) * block), clear, tiles * 256, reach_of(places, first, second)

    last = [reach_of(offset + (n + 1) * block - 1, first, second) for n in range(count)]
    for begin in range(0, count, per):
        group = range(begin, min(begin + per, count))
        for tiles in itertools.product(*[options(n) for n in group]):
            fits = [(last[n] >= (t - 1) * 256) & (last[n] < t * 256) for n, t in zip(group, tiles)]

            @pl.when(functools.reduce(jnp.logical_and, fits))
            def _(group=group, tiles=tiles):
                run([item(n, t) for n, t in zip(group, tiles)])


def hide(scores, clear, reach):
    span, block = scores.shape
    places = clear + lax.broadcasted_iota(jnp.int32, (span - clear, block), 0)
    tail = jnp.where(places <= reach, scores[clear:], NEGATIVE)
    return tail if clear == 0 else jnp.concatenate([scores[:clear], tail], axis=0)


def head_masks():
    lanes = lax.broadcasted_iota(jnp.int32, (1, 2 * HEAD_DIM), 1)
    return [lanes < HEAD_DIM, lanes >= HEAD_DIM]


def pick(mask, values):
    return jnp.where(mask, values, jnp.zeros_like(values))


def staggered(count, ahead, start, finish):
    for i in range(min(ahead, count)):
        start(i)
    for i in range(count):
        if i + ahead < count:
            start(i + ahead)
        finish(i)


POWER = SCALE * LOG2E
SAFE = 2.0**100


def attend_body(fixed_offset, starts_ref, offset_ref, q_ref, k_ref, v_ref, out_ref, lse_ref, vt_ref, worst_ref):
    masks = head_masks()
    queries, keys = q_ref.shape[1], k_ref.shape[1]
    pairs = q_ref.shape[2] // 128
    for p in range(pairs):
        vt_ref[p * 128 : (p + 1) * 128, :] = v_ref[0, :, p * 128 : (p + 1) * 128].T
    worst_ref[...] = jnp.zeros_like(worst_ref)

    def run(exact, items):
        units = [(it, p, h) for it in items for p in range(pairs) for h in range(2)]
        held = [None] * len(units)

        def start(i):
            (at, clear, span, reach), p, h = units[i]
            lanes = slice(p * 128, (p + 1) * 128)
            held[i] = hide(dot(k_ref[0, :span, lanes], pick(masks[h], q_ref[0, at, lanes]), NT), clear, reach)

        def finish(i):
            (at, _, span, _), p, h = units[i]
            s = held[i]
            top = jnp.max(s, axis=0, keepdims=True) if exact else s[:1]
            raised = jnp.exp2((s - top) * POWER)
            size = jnp.sum(raised, axis=0, keepdims=True)
            if not exact:
                worst_ref[...] = jnp.maximum(worst_ref[...], size)
            lse_ref[0, p, h : h + 1, at] = top * POWER + jnp.log2(size)
            mine = slice(p * 128 + h * HEAD_DIM, p * 128 + (h + 1) * HEAD_DIM)
            total = dot(vt_ref[mine, :span], raised.astype(BF), NN)
            out_ref[mine, at] = (total * (1.0 / size)).astype(BF)

        staggered(len(units), 2, start, finish)

    args = (starts_ref, offset_ref, queries, keys, fixed_offset)
    query_groups(*args, 2, functools.partial(run, False))

    @pl.when(jnp.max(worst_ref[...]) >= SAFE)
    def _():
        query_groups(*args, 1, functools.partial(run, True))


def attend(starts, offset, q, k, v, fixed_offset):
    count, queries, d = q.shape
    keys = k.shape[1]
    lanes = 256
    rows = lambda n: pl.BlockSpec((1, n, lanes), lambda b, p, *_: (b, 0, p))
    return pl.pallas_call(
        functools.partial(attend_body, fixed_offset),
        grid_spec=pltpu.PrefetchScalarGridSpec(
            num_scalar_prefetch=2,
            grid=(count, d // lanes),
            in_specs=[rows(queries), rows(keys), rows(keys)],
            out_specs=[
                pl.BlockSpec((lanes, queries), lambda b, p, *_: (p, b)),
                pl.BlockSpec((1, lanes // 128, 2, queries), lambda b, p, *_: (b, p, 0, 0)),
            ],
            scratch_shapes=[pltpu.VMEM((lanes, keys), BF), pltpu.VMEM((1, min(256, queries)), F32)],
        ),
        out_shape=[shape((d, count * queries), BF), shape((count, d // 128, 2, queries), F32)],
        compiler_params=params(),
        cost_estimate=cost(12 * count * queries * keys * d, 8 * count * keys * d, count * d // 64 * queries * keys),
        name="attend",
    )(starts, offset, q, k, v)


def attend_back_body(
    fixed_offset, starts_ref, offset_ref, q_ref, k_ref, v_ref, g_ref, att_ref, lse_ref,
    dq_ref, dkv_ref, kt_ref, settled_ref, dk_acc, dv_acc,
):
    masks = head_masks()
    queries, keys = q_ref.shape[1], k_ref.shape[1]
    pairs = q_ref.shape[2] // 128
    dk_acc[...] = jnp.zeros_like(dk_acc)
    dv_acc[...] = jnp.zeros_like(dv_acc)
    for p in range(pairs):
        lanes = slice(p * 128, (p + 1) * 128)
        kt_ref[lanes, :] = k_ref[0, :, lanes].T
        both = g_ref[0, :, lanes].T.astype(F32) * att_ref[lanes, :].astype(F32)
        for h in range(2):
            part = both[h * HEAD_DIM : (h + 1) * HEAD_DIM]
            settled_ref[2 * p + h : 2 * p + h + 1, :] = jnp.sum(part, axis=0, keepdims=True)

    def run(items):
        units = [(it, p, h) for it in items for p in range(pairs) for h in range(2)]
        held = [None] * len(units)
        done = {}

        def start(i):
            (at, clear, span, reach), p, h = units[i]
            lanes = slice(p * 128, (p + 1) * 128)
            q, g = pick(masks[h], q_ref[0, at, lanes]), pick(masks[h], g_ref[0, at, lanes])
            s = hide(dot(k_ref[0, :span, lanes], q, NT), clear, reach)
            held[i] = (s, dot(v_ref[0, :span, lanes], g, NT), q, g)

        def finish(i):
            (at, _, span, _), p, h = units[i]
            s, chance_grad, q, g = held[i]
            n = 2 * p + h
            chances = jnp.exp2(s * POWER - lse_ref[0, p, h : h + 1, at])
            ds = (chances * (chance_grad - settled_ref[n : n + 1, at])).astype(BF)
            dq = dot(kt_ref[n * HEAD_DIM : (n + 1) * HEAD_DIM, :span], ds, NN)
            done[h] = (chances.astype(BF), ds, q, g, dq)
            if h == 1:
                lanes = slice(p * 128, (p + 1) * 128)
                join = lambda m, axis: jnp.concatenate([done[0][m], done[1][m]], axis=axis)
                dv_acc[:span, lanes] += dot(join(0, 1), join(3, 0), NN)
                dk_acc[:span, lanes] += dot(join(1, 1), join(2, 0), NN)
                dq_ref[0, at, lanes] = (join(4, 0).T * SCALE).astype(BF)

        staggered(len(units), 2, start, finish)

    query_groups(starts_ref, offset_ref, queries, keys, fixed_offset, 2, run)
    dkv_ref[0, 0] = (dk_acc[...] * SCALE).astype(BF)
    dkv_ref[1, 0] = dv_acc[...].astype(BF)


def attend_back(starts, offset, q, k, v, g, att, lse, fixed_offset):
    count, queries, d = q.shape
    keys = k.shape[1]
    lanes = 256
    rows = lambda n: pl.BlockSpec((1, n, lanes), lambda b, p, *_: (b, 0, p))
    return pl.pallas_call(
        functools.partial(attend_back_body, fixed_offset),
        grid_spec=pltpu.PrefetchScalarGridSpec(
            num_scalar_prefetch=2,
            grid=(count, d // lanes),
            in_specs=[
                rows(queries),
                rows(keys),
                rows(keys),
                rows(queries),
                pl.BlockSpec((lanes, queries), lambda b, p, *_: (p, b)),
                pl.BlockSpec((1, lanes // 128, 2, queries), lambda b, p, *_: (b, p, 0, 0)),
            ],
            out_specs=[
                rows(queries),
                pl.BlockSpec((2, 1, keys, lanes), lambda b, p, *_: (0, b, 0, p)),
            ],
            scratch_shapes=[
                pltpu.VMEM((lanes, keys), BF),
                pltpu.VMEM((lanes // HEAD_DIM, queries), F32),
                pltpu.VMEM((keys, lanes), F32),
                pltpu.VMEM((keys, lanes), F32),
            ],
        ),
        out_shape=[shape((count, queries, d), BF), shape((2, count, keys, d), BF)],
        compiler_params=params(),
        cost_estimate=cost(30 * count * queries * keys * d, 14 * count * keys * d, count * d // 64 * queries * keys),
        name="attend_back",
    )(starts, offset, q, k, v, g, att, lse)


def hidden_chunk(up_ref):
    return min(512, up_ref.shape[3])


def up_chunk(up_ref, n, size):
    per = up_ref.shape[3] // size
    block = up_ref[:, n // per, :, (n % per) * size : (n % per + 1) * size]
    return block.reshape(block.shape[0] * block.shape[1], size)


def settle_body(x_ref, att_ref, vec_ref, wo_ref, mid_ref, x2_ref):
    att = att_ref[...]
    parts = [dot(att, weight_columns(wo_ref, j), TN) for j in range(wo_ref.shape[1])]
    branch = jnp.concatenate(parts, axis=1)
    middle = x_ref[...].astype(F32) + (branch + row(vec_ref, OUTPUT_BIAS))
    mid_ref[...] = middle
    hat, _ = norm_parts(middle)
    x2_ref[...] = (hat * row(vec_ref, GAIN_TWO) + row(vec_ref, SHIFT_TWO)).astype(BF)


def settle(x, att, vec, first, tile):
    tokens, d = x.shape
    dp, g, _, width = first.shape
    per = d // dp
    tok = pl.BlockSpec((tile, d), lambda i: (i, 0))
    return pl.pallas_call(
        settle_body,
        grid=(tokens // tile,),
        in_specs=[
            tok,
            pl.BlockSpec((d, tile), lambda i: (0, i)),
            once((8, d), lambda i: (0, 0)),
            once((dp, g, per, width), lambda i: (0, 0, 3, 0)),
        ],
        out_specs=[tok, tok],
        out_shape=[shape((tokens, d), F32), shape((tokens, d), BF)],
        compiler_params=params(),
        cost_estimate=cost(2 * tokens * d * d, 10 * tokens * d + 2 * d * d),
        name="settle",
    )(x, att, vec, first)


def rise_body(x2_ref, upb_ref, up_ref, act_ref, slope_ref):
    x2 = x2_ref[...]
    size = hidden_chunk(up_ref)
    for n in range(up_ref.shape[1] * up_ref.shape[3] // size):
        at = slice(n * size, (n + 1) * size)
        x = dot(x2, up_chunk(up_ref, n, size), NN) + upb_ref[:, at]
        square = x * x
        half = 0.5 + 0.5 * jnp.tanh(x * (BENDING + (BENDING * CUBIC_TERM) * square))
        act_ref[:, at] = (x * half).astype(BF)
        bend = x * (2.0 * BENDING + (6.0 * BENDING * CUBIC_TERM) * square)
        slope_ref[:, at] = (half + half * (1.0 - half) * bend).astype(BF)


def rise(x2, upb, up, tile):
    tokens, d = x2.shape
    ff = upb.shape[1]
    wide = pl.BlockSpec((tile, ff), lambda i: (i, 0))
    return pl.pallas_call(
        rise_body,
        grid=(tokens // tile,),
        in_specs=[
            pl.BlockSpec((tile, d), lambda i: (i, 0)),
            once((1, ff), lambda i: (0, 0)),
            once(up.shape, lambda i: (0, 0, 0, 0)),
        ],
        out_specs=[wide, wide],
        out_shape=[shape((tokens, ff), BF), shape((tokens, ff), BF)],
        compiler_params=params(),
        cost_estimate=cost(2 * tokens * d * ff, tokens * (2 * d + 4 * ff) + 2 * d * ff, tokens * ff),
        name="rise",
    )(x2, upb, up)


def fall_body(
    begun, which_ref, mid_ref, act_ref, slope_ref, og_ref, vec_ref, wo_ref, up_ref, down_ref, *rest
):
    out_ref, bg_ref, mg_ref, br_ref, dat_ref, upb_ref, sums_ref = rest[4:] if begun else rest
    clear_at_start(upb_ref, sums_ref)
    og = og_ref[...]
    incoming = og.astype(F32)
    g, width = down_ref.shape[1], down_ref.shape[3]
    size = hidden_chunk(up_ref)
    per = size // down_ref.shape[2]
    chunks = up_ref.shape[1] * up_ref.shape[3] // size
    outs = [None] * g
    e = None
    for n in range(chunks):
        at = slice(n * size, (n + 1) * size)
        act = act_ref[:, at]
        rise_grad = None
        for j in range(g):
            block = down_ref[n * per : (n + 1) * per, j].reshape(size, width)
            part = dot(og[:, j * width : (j + 1) * width], block, NT)
            rise_grad = part if rise_grad is None else rise_grad + part
            part = dot(act, block, NN)
            outs[j] = part if outs[j] is None else outs[j] + part
        bg = (slope_ref[:, at].astype(F32) * rise_grad).astype(BF)
        bg_ref[:, at] = bg
        upb_ref[:, at] += fold(bg.astype(F32))
        part = dot(bg, up_chunk(up_ref, n, size), NT)
        e = part if e is None else e + part
    middle = mid_ref[...]
    out_ref[...] = (middle + (jnp.concatenate(outs, axis=1) + row(vec_ref, DOWN_BIAS))).astype(BF)
    hat, inverse = norm_parts(middle)
    middle_grad = incoming + norm_back(e, hat, inverse, row(vec_ref, GAIN_TWO))
    mg_ref[...] = middle_grad
    branch = middle_grad.astype(BF)
    br_ref[...] = branch
    back = None
    for j in range(wo_ref.shape[1]):
        part = dot(branch[:, j * width : (j + 1) * width], weight_columns(wo_ref, j), NT)
        back = part if back is None else back + part
    dat_ref[...] = back.astype(BF)
    sums_ref[0] += fold(e * hat)
    sums_ref[1] += fold(e)
    sums_ref[2] += fold(branch.astype(F32))
    sums_ref[3] += fold(incoming)


def fall(middle, act, slope, og, vec, first, up, down, tile, which, sequences, halves, begun=()):
    tokens, d = og.shape
    dp, g, _, width = first.shape
    per = d // dp
    ff = act.shape[1]
    per_half = tokens // tile // sequences // halves
    kept = tokens // halves

    def block(i, w):
        return (i // per_half) * (per_half * halves) + w[0] * per_half + i % per_half, 0

    tok = pl.BlockSpec((tile, d), block)
    wide = pl.BlockSpec((tile, ff), block)
    fixed = lambda dims: once(dims, lambda i, w: (0,) * len(dims))
    return pl.pallas_call(
        functools.partial(fall_body, bool(begun)),
        grid_spec=pltpu.PrefetchScalarGridSpec(
            num_scalar_prefetch=1,
            grid=(kept // tile,),
            in_specs=[
                tok, wide, wide, tok,
                fixed((8, d)),
                once((dp, g, per, width), lambda i, w: (0, 0, 3, 0)),
                fixed(up.shape),
                fixed(down.shape),
            ] + [pl.BlockSpec(memory_space=pl.ANY)] * len(begun),
            out_specs=[
                pl.BlockSpec((tile, d), lambda i, w: (i, 0)), wide, tok, tok, tok,
                pl.BlockSpec((8, ff), lambda i, w: (0, 0)),
                pl.BlockSpec((4, 8, d), lambda i, w: (0, 0, 0)),
            ],
        ),
        out_shape=[
            shape((kept, d), BF), shape((tokens, ff), BF), shape((tokens, d), F32), shape((tokens, d), BF),
            shape((tokens, d), BF), shape((8, ff), F32), shape((4, 8, d), F32),
        ],
        input_output_aliases={9 + n: 1 + n for n in range(len(begun))},
        compiler_params=params(),
        cost_estimate=cost(2 * kept * d * (d + 3 * ff), kept * (16 * d + 6 * ff) + 2 * d * (d + 2 * ff)),
        name="fall",
    )(which, middle, act, slope, og, vec, first, up, down, *begun)


def split_cores(core_ref, values, keep_ref, send_ref):
    even, odd = values[:, 0], values[:, 1]
    mine = core_ref[0] == 0
    keep_ref[...] = jnp.where(mine, even, odd).astype(BF)
    send_ref[...] = jnp.where(mine, odd, even).astype(BF)


def down_grad_body(core_ref, act_ref, og_ref, keep_ref, send_ref):
    y = dot(act_ref[...], og_ref[...], TN)
    chips, g, rows, width = keep_ref.shape
    for j in range(g):
        part = y[:, j * width : (j + 1) * width].reshape(chips, 2, rows, width)
        split_cores(core_ref, part, keep_ref.at[:, j], send_ref.at[:, j])


def down_grad(core, act, og, dp, g):
    tokens, ff = act.shape
    d = og.shape[1]
    size = min(512, ff)
    rows, width = ff // dp, d // g
    chips = size // rows // 2
    out = pl.BlockSpec((chips, g, rows, width), lambda i, *_: (i, 0, 0, 0))
    return pl.pallas_call(
        down_grad_body,
        grid_spec=pltpu.PrefetchScalarGridSpec(
            num_scalar_prefetch=1,
            grid=(ff // size,),
            in_specs=[pl.BlockSpec((tokens, size), lambda i, *_: (0, i)), once((tokens, d), lambda i, *_: (0, 0))],
            out_specs=[out, out],
        ),
        out_shape=[shape((dp // 2, g, rows, width), BF)] * 2,
        compiler_params=params(),
        cost_estimate=cost(2 * tokens * d * ff, 2 * (tokens * (d + ff) + d * ff)),
        name="down_grad",
    )(core, act, og)


def weight_grad_body(form, core_ref, x_ref, dy_ref, keep_ref, send_ref):
    dy = dy_ref[...]
    y = dot(x_ref[...], dy.reshape(dy.shape[-2:]), form)
    chips, _, rows, width = keep_ref.shape
    split_cores(core_ref, y.reshape(chips, 2, rows, width), keep_ref.at[:, 0], send_ref.at[:, 0])


def weight_grad(core, x, dy, dp, g, form, name):
    count, tokens, columns = dy.shape
    d = x.shape[0] if form == NN else x.shape[1]
    share = columns // g
    size = min(512, share)
    per = share // size
    rows = d // dp
    out = pl.BlockSpec((dp // 2, 1, rows, size), lambda m, i, *_: (0, i // per, m, i % per))
    return pl.pallas_call(
        functools.partial(weight_grad_body, form),
        grid_spec=pltpu.PrefetchScalarGridSpec(
            num_scalar_prefetch=1,
            grid=(count, columns // size),
            in_specs=[
                once(x.shape, lambda m, i, *_: (0, 0)),
                pl.BlockSpec((1, tokens, size), lambda m, i, *_: (m, 0, i)),
            ],
            out_specs=[out, out],
        ),
        out_shape=[shape((dp // 2, g, count * rows, share), BF)] * 2,
        compiler_params=params(),
        cost_estimate=cost(2 * count * tokens * d * columns, 2 * (tokens * d + count * columns * (tokens + d))),
        name=name,
    )(core, x, dy)


def input_body(which_ref, x_ref, mg_ref, dq_ref, dkv_ref, vec_ref, w_ref, out_ref, sums_ref):
    clear_at_start(sums_ref)
    groups, per, width = w_ref.shape[1], w_ref.shape[2] // 3, w_ref.shape[3]
    e = None
    grads = (dq_ref[...], dkv_ref[0], dkv_ref[1])
    for m in range(3):
        for j in range(groups):
            at = slice(j * width, (j + 1) * width)
            part = dot(grads[m][:, at], weight_columns(w_ref, j, slice(m * per, (m + 1) * per)), NT)
            e = part if e is None else e + part
    hat, inverse = norm_parts(x_ref[...].astype(F32))
    out_ref[...] = (mg_ref[...] + norm_back(e, hat, inverse, row(vec_ref, GAIN_ONE))).astype(BF)
    sums_ref[0] += fold(e * hat)
    sums_ref[1] += fold(e)
    sums_ref[2] += fold(grads[0].astype(F32))
    sums_ref[3] += fold(grads[2].astype(F32))


def input_back(x, mg, dq, dkv, vec, first, tile, which, sequences, halves):
    tokens, d = x.shape
    dp, g, rows, width = first.shape
    per = d // dp
    per_half = tokens // tile // sequences // halves

    def block(i, which):
        return (i // per_half) * (per_half * halves) + which[0] * per_half + i % per_half

    tok = pl.BlockSpec((tile, d), lambda i, w: (block(i, w), 0))
    kept = tokens // halves
    return pl.pallas_call(
        input_body,
        grid_spec=pltpu.PrefetchScalarGridSpec(
            num_scalar_prefetch=1,
            grid=(kept // tile,),
            in_specs=[
                tok, tok, tok,
                pl.BlockSpec((2, tile, d), lambda i, w: (0, block(i, w), 0)),
                once((8, d), lambda i, w: (0, 0)),
                once((dp, g, 3 * per, width), lambda i, w: (0, 0, 0, 0)),
            ],
            out_specs=[
                pl.BlockSpec((tile, d), lambda i, w: (i, 0)),
                pl.BlockSpec((4, 8, d), lambda i, w: (0, 0, 0)),
            ],
        ),
        out_shape=[shape((kept, d), BF), shape((4, 8, d), F32)],
        compiler_params=params(),
        cost_estimate=cost(6 * kept * d * d, 16 * kept * d + 6 * d * d),
        name="input_back",
    )(which, x, mg, dq, dkv, vec, first)


def swap_cores(values):
    return lax.ppermute(values, "core", [(0, 1), (1, 0)])


def add_cores(keep, send):
    return (keep.astype(F32) + swap_cores(send).astype(F32)).astype(BF)


def add_chips(mine):
    chips, g = mine.shape[:2]
    flat = mine.reshape((chips * g,) + mine.shape[2:])
    return lax.psum_scatter(flat, ("z", "x", "seq"), scatter_dimension=0, tiled=True)[0].astype(F32)


NEAR = ("z", [(0, 1), (1, 0), (2, 3), (3, 2)])
FAR = ("z", [(0, 2), (2, 0), (1, 3), (3, 1)])
ACROSS = ("x", [(0, 1), (1, 0)])
ALONG = ("seq", [(0, 1), (1, 0)])


def cut(values, dim, own, route):
    keep = lax.dynamic_index_in_dim(values, own, dim, keepdims=False)
    return keep, lax.dynamic_index_in_dim(values, 1 - own, dim, keepdims=False), route


def add_step(step, came):
    return (step[0].astype(F32) + came.astype(F32)).astype(BF)


def halve(values, dim, own, route):
    step = cut(values, dim, own, route)
    return add_step(step, lax.ppermute(step[1], *route))


def start_step(mine, across_first):
    values = mine.reshape((2, 2, 2) + mine.shape[1:])
    if across_first:
        return cut(values, 2, lax.axis_index("x"), ACROSS)
    return cut(values, 1, lax.axis_index("z") % 2, NEAR)


def next_step(values, across_first):
    if across_first:
        return cut(values, 1, lax.axis_index("z") % 2, NEAR)
    return cut(values, 0, lax.axis_index("z") // 2, FAR)


def last_steps(values, across_first):
    if across_first:
        values = halve(values, 0, lax.axis_index("z") // 2, FAR)
    else:
        values = halve(values, 0, lax.axis_index("x"), ACROSS)
    return halve(values, 0, lax.axis_index("seq"), ALONG).astype(F32)


def all_steps(mine):
    step = start_step(mine, True)
    step = next_step(add_step(step, lax.ppermute(step[1], *step[2])), True)
    return last_steps(add_step(step, lax.ppermute(step[1], *step[2])), True)


def body(
    tokens, first_gain, first_shift, query_weight, query_bias, key_weight, value_weight, value_bias,
    output_weight, output_bias, second_gain, second_shift, up_weight, up_bias, down_weight, down_bias,
    piece_starts, out_grad,
):
    chips, g = lax.axis_size("z") * lax.axis_size("x"), lax.axis_size("seq")
    dp = 2 * chips
    everyone = ("z", "x", "core", "seq")
    count, local, d = tokens.shape
    width = query_weight.shape[1]
    per = query_weight.shape[0]
    small = first_gain.shape[0]
    wide = up_bias.shape[0]
    ff = wide * dp * g
    length = local * g
    place = lax.axis_index("seq")
    core = lax.axis_index("core").astype(jnp.int32).reshape(1)
    paired = g == 2 and count % 2 == 0

    vectors = [first_gain, first_shift, query_bias, value_bias, output_bias, second_gain, second_shift, down_bias]
    extra = 16
    packed = pack([query_weight, key_weight, value_weight, output_weight], vectors + [up_bias], extra)
    first = lax.all_gather(packed, everyone, axis=0).reshape(dp, g, 4 * per + extra, width)
    up = lax.all_gather(up_weight, everyone, axis=0).reshape((dp, g) + up_weight.shape)
    down = lax.all_gather(down_weight, everyone, axis=0).reshape((dp, g) + down_weight.shape)

    if paired:
        half = count // 2

        def swap_rows(values, *earlier):
            sent = lax.dynamic_slice_in_dim(values, (1 - place) * half, half, 0)
            return lax.ppermute(after(sent, *earlier), "seq", [(0, 1), (1, 0)])

        def gather_rows(values, came):
            kept = lax.dynamic_slice_in_dim(values, place * half, half, 0)
            low = jnp.where(place == 0, kept, came)
            high = jnp.where(place == 0, came, kept)
            return jnp.concatenate([low, high], axis=1).reshape(half * length, d)

        def join_rows(kept, came):
            low = jnp.where(place == 0, kept, came)
            high = jnp.where(place == 0, came, kept)
            return jnp.concatenate([low, high], axis=0)

        starts = lax.dynamic_slice_in_dim(piece_starts, place * half, half, 0)
        offset = jnp.zeros((1,), jnp.int32)
        sequences, queries = half, length
    else:
        swap_rows = lambda values, *earlier: values
        gather_rows = lambda values, came: values.reshape(count * local, d)
        starts = piece_starts
        offset = (place * local).astype(jnp.int32).reshape(1)
        sequences, queries = count, local

    rows = sequences * queries
    tile = min(256, rows)
    x = gather_rows(tokens, swap_rows(tokens))
    first = after(first, x)
    vec = first[:, :, 4 * per : 4 * per + 8, :small].astype(F32).transpose(2, 0, 1, 3).reshape(8, d)
    upb = first[:, :, 4 * per + 8, :wide].astype(F32).reshape(1, ff)
    came = swap_rows(out_grad, first)
    x1, q, k, v = project(x, vec, first, tile)
    q, k, v = (t.reshape(sequences, queries, d) for t in (q, k, v))
    if not paired:
        k, v = (lax.all_gather(t, "seq", axis=1, tiled=True) for t in (k, v))
    att, lse = attend(starts, offset, q, k, v, paired)
    og = gather_rows(out_grad, after(came, att))
    middle, x2 = settle(x, att, vec, first, tile)
    act, slope = rise(after(x2, og), upb, up, min(512, rows))
    down_mine = add_cores(*down_grad(core, act, og, dp, g))
    down_sum = add_chips(down_mine)
    act = after(act, down_mine)
    args = (middle, act, slope, og, vec, first, up, down, tile)
    if paired:
        turn = place.astype(jnp.int32).reshape(1)
        out_sent, *begun, upb_sent, two_sent = fall(*args, 1 - turn, sequences, 2)
        out, *begun, upb_sums, sums_two = fall(*args, turn, sequences, 2, tuple(begun))
        bg, mg, branch, dat = begun
        upb_sums, sums_two = upb_sums + upb_sent, sums_two + two_sent
        came_out = lax.ppermute(out_sent.reshape(half, local, d), *ALONG)
    else:
        out, bg, mg, branch, dat, upb_sums, sums_two = fall(*args, jnp.zeros((1,), jnp.int32), sequences, 1)
        output = out.reshape(count, local, d)
    up_parts = weight_grad(core, x2, bg[None], dp, g, TN, "up_grad")
    out_parts = weight_grad(core, att, branch[None], dp, g, NN, "out_grad")
    if paired:
        up_parts, out_parts, came_out = lax.optimization_barrier((up_parts, out_parts, came_out))
        output = join_rows(out.reshape(half, local, d), came_out)
    up_mine = jnp.concatenate([add_cores(*up_parts), add_cores(*out_parts)], axis=-1)
    up_sum = add_chips(up_mine)
    dat = after(dat, up_mine, down_sum)
    dq, dkv = attend_back(starts, offset, q, k, v, dat.reshape(sequences, queries, d), att, lse, paired)
    dq = dq.reshape(rows, d)
    if not paired:
        dkv = lax.psum_scatter(dkv, "seq", scatter_dimension=2, tiled=True)
    dkv = dkv.reshape(2, rows, d)
    query_parts = weight_grad(core, x1, dq[None], dp, g, TN, "query_grad")
    kv_parts = weight_grad(core, x1, dkv, dp, g, TN, "key_value_grad")
    query_mine, kv_mine = add_cores(*query_parts), add_cores(*kv_parts)
    first_parts = jnp.concatenate([query_mine, kv_mine[:, :, :per]], axis=2)
    second_parts = kv_mine[:, :, per:]
    stepwise = (lax.axis_size("z"), lax.axis_size("x"), g) == (4, 2, 2)
    dkv = after(dkv, first_parts, second_parts, up_sum)
    args = (x, mg, dq, dkv, vec, first, tile)
    if paired:
        sent, sums_sent = input_back(*args, 1 - turn, sequences, 2)
        came_in = lax.ppermute(sent.reshape(half, local, d), *ALONG)
        if stepwise:
            steps = [start_step(first_parts, True), start_step(second_parts, False)]
            arrived = [after(lax.ppermute(move, *route), sent) for _, move, route in steps]
            steps = [next_step(add_step(step, move), n == 0) for n, (step, move) in enumerate(zip(steps, arrived))]
            arrived = [lax.ppermute(move, *route) for _, move, route in steps]
            args = args[:3] + (after(dkv, steps[0][1], steps[1][1]),) + args[4:]
        in_grad, sums_one = input_back(*args, turn, sequences, 2)
        if stepwise:
            arrived[0], arrived[1], came_in, sums_one = lax.optimization_barrier((*arrived, came_in, sums_one))
            summed = [add_step(step, move) for step, move in zip(steps, arrived)]
        sums_one = sums_one + sums_sent
        came_in = lax.ppermute(sent.reshape(half, local, d), "seq", [(0, 1), (1, 0)])
        input_grad = join_rows(in_grad.reshape(half, local, d), came_in)
    else:
        in_grad, sums_one = input_back(*args, jnp.zeros((1,), jnp.int32), sequences, 1)
        input_grad = in_grad.reshape(count, local, d)

    one, two = jnp.sum(sums_one, axis=1), jnp.sum(sums_two, axis=1)
    eight = jnp.stack([one[0], one[1], one[2], one[3], two[2], two[0], two[1], two[3]])
    eight = eight.reshape(8, chips, 2, g, small).transpose(2, 1, 3, 0, 4).reshape(2, chips, g, 8 * small)
    upb_grad = jnp.sum(upb_sums, axis=0).reshape(chips, 2, g, wide).transpose(1, 0, 2, 3)
    lines = jnp.concatenate([eight, upb_grad], axis=-1)
    lines = jnp.pad(lines, ((0, 0), (0, 0), (0, 0), (0, extra * width - lines.shape[-1])))
    lines = lines.reshape(2, chips, g, extra, width).astype(BF)
    own = lax.axis_index("core")
    line_mine = add_cores(
        lax.dynamic_index_in_dim(lines, own, 0, keepdims=False),
        lax.dynamic_index_in_dim(lines, 1 - own, 0, keepdims=False),
    )
    if stepwise:
        last = [last_steps(summed[0], True), last_steps(summed[1], False), all_steps(line_mine)]
        last = jnp.concatenate(last, axis=0)
    else:
        last = add_chips(jnp.concatenate([first_parts, second_parts, line_mine], axis=2))
    dw = [last[m * per : (m + 1) * per] for m in range(3)] + [up_sum[:, -width:]]
    up_sum = up_sum[:, :-width]
    line = last[3 * per :].reshape(extra * width)
    grads = [line[m * small : (m + 1) * small] for m in range(8)]
    gain_one, shift_one, query_add, value_add, output_add, gain_two, shift_two, down_add = grads
    up_add = line[8 * small : 8 * small + wide]
    return (
        output, input_grad, gain_one, shift_one, dw[0], query_add, dw[1], dw[2], value_add, dw[3], output_add,
        gain_two, shift_two, up_sum, up_add, down_sum, down_add,
    )


def solution(mesh):
    dp, g = mesh.shape["dp"], mesh.shape["seq"]
    fine = Mesh(mesh.devices.reshape(4, dp // 8, 2, g), ("z", "x", "core", "seq"))
    both = ("z", "x", "core")
    rows, vector, matrix = P(both, "seq", None), P(both + ("seq",)), P(both, "seq")
    in_specs = (
        rows, vector, vector, matrix, vector, matrix, matrix, vector, matrix, vector, vector, vector, matrix,
        vector, matrix, vector, P(both, None), rows,
    )
    out_specs = (
        rows, rows, vector, vector, matrix, vector, matrix, matrix, vector, matrix, vector, vector, vector,
        matrix, vector, matrix, vector,
    )
    return jax.shard_map(body, mesh=fine, in_specs=in_specs, out_specs=out_specs, check_vma=False)
```

```python
import functools
import itertools
import math

import jax
import jax.numpy as jnp
from jax import lax
from jax.experimental import pallas as pl
from jax.experimental.pallas import tpu as pltpu
from jax.sharding import Mesh, PartitionSpec as P

HEAD_DIM = 64
PIECE = 256
NEGATIVE = -1e30
EPSILON = 1e-05
BENDING = math.sqrt(2.0 / math.pi)
CUBIC_TERM = 0.044715
SCALE = HEAD_DIM**-0.5
LOG2E = math.log2(math.e)

BF = jnp.bfloat16
F32 = jnp.float32
VMEM_LIMIT = 60 * 2**20
COST_PARTS = 1

NN = (((1,), (0,)), ((), ()))
NT = (((1,), (1,)), ((), ()))
TN = (((0,), (0,)), ((), ()))


def dot(left, right, form):
    return lax.dot_general(left, right, form, preferred_element_type=F32)


def params():
    return pltpu.CompilerParams(vmem_limit_bytes=VMEM_LIMIT)


def cost(flops, nbytes, trans=0):
    part = lambda n: int(n) // COST_PARTS
    return pl.CostEstimate(flops=part(flops), bytes_accessed=part(nbytes), transcendentals=part(trans))


def shape(dims, dtype):
    return jax.ShapeDtypeStruct(dims, dtype)


def once(block, index):
    return pl.BlockSpec(block, index, pipeline_mode=pl.Buffered(1))


def after(values, *earlier):
    return lax.optimization_barrier((values,) + earlier)[0]


def norm_parts(values):
    centre = values - jnp.mean(values, axis=-1, keepdims=True)
    inverse = lax.rsqrt(jnp.mean(centre * centre, axis=-1, keepdims=True) + EPSILON)
    return centre * inverse, inverse


def norm_back(upstream, hat, inverse, gain):
    scaled = upstream * gain
    return inverse * (
        scaled
        - jnp.mean(scaled, axis=-1, keepdims=True)
        - hat * jnp.mean(scaled * hat, axis=-1, keepdims=True)
    )


def fold(values):
    rows, columns = values.shape
    return jnp.sum(values.reshape(rows // 8, 8, columns), axis=0)


def clear_at_start(*refs):
    @pl.when(pl.program_id(0) == 0)
    def _():
        for ref in refs:
            ref[...] = jnp.zeros_like(ref)


GAIN_ONE, SHIFT_ONE, QUERY_BIAS, VALUE_BIAS, OUTPUT_BIAS, GAIN_TWO, SHIFT_TWO, DOWN_BIAS = range(8)


def row(ref, index):
    return ref[index : index + 1, :]


def weight_columns(ref, j, rows=slice(None)):
    block = ref[:, j, rows, :]
    return block.reshape(block.shape[0] * block.shape[1], block.shape[2])


def pack_body(*refs):
    out = refs[-1]
    out[...] = jnp.zeros_like(out)
    at = 0
    for ref in refs[:-1]:
        out[at : at + ref.shape[0], : ref.shape[1]] = ref[...]
        at += ref.shape[0]


def pack(matrices, vectors, extra):
    rows = sum(m.shape[0] for m in matrices) + extra
    return pl.pallas_call(
        pack_body,
        out_shape=shape((rows, matrices[0].shape[1]), BF),
        compiler_params=params(),
        name="pack",
    )(*matrices, *[v.reshape(1, -1) for v in vectors])


def project_body(x_ref, vec_ref, w_ref, x1_ref, q_ref, k_ref, v_ref):
    hat, _ = norm_parts(x_ref[...].astype(F32))
    x1 = (hat * row(vec_ref, GAIN_ONE) + row(vec_ref, SHIFT_ONE)).astype(BF)
    x1_ref[...] = x1
    groups, per, width = w_ref.shape[1], w_ref.shape[2] // 3, w_ref.shape[3]
    for m, (out, bias) in enumerate(((q_ref, QUERY_BIAS), (k_ref, None), (v_ref, VALUE_BIAS))):
        for j in range(groups):
            at = slice(j * width, (j + 1) * width)
            y = dot(x1, weight_columns(w_ref, j, slice(m * per, (m + 1) * per)), NN)
            if bias is not None:
                y = y + vec_ref[bias : bias + 1, at]
            out[:, at] = y.astype(BF)


def project(x, vec, first, tile):
    tokens, d = x.shape
    dp, g, rows, width = first.shape
    per = d // dp
    tok = pl.BlockSpec((tile, d), lambda i: (i, 0))
    return pl.pallas_call(
        project_body,
        grid=(tokens // tile,),
        in_specs=[tok, once((8, d), lambda i: (0, 0)), once((dp, g, 3 * per, width), lambda i: (0, 0, 0, 0))],
        out_specs=[tok] * 4,
        out_shape=[shape((tokens, d), BF)] * 4,
        compiler_params=params(),
        cost_estimate=cost(6 * tokens * d * d, 10 * tokens * d + 6 * d * d),
        name="project",
    )(x, vec, first)


def reach_of(places, first, second):
    in_first = (places >= first) & (places < first + PIECE)
    in_second = (places >= second) & (places < second + PIECE)
    return jnp.where(in_first, first + (PIECE - 1), jnp.where(in_second, second + (PIECE - 1), places))


def query_groups(starts_ref, offset_ref, queries, keys, fixed_offset, per, run):
    b = pl.program_id(0)
    first, second = starts_ref[b, 0], starts_ref[b, 1]
    offset = offset_ref[0]
    block = min(256, queries)
    count = queries // block

    def options(n):
        return range(n + 1, min(n + 2, keys // 256) + 1) if fixed_offset else range(1, keys // 256 + 1)

    def item(n, tiles):
        places = offset + n * block + lax.broadcasted_iota(jnp.int32, (1, block), 1)
        clear = n * 256 if fixed_offset else 0
        return slice(n * block, (n + 1) * block), clear, tiles * 256, reach_of(places, first, second)

    last = [reach_of(offset + (n + 1) * block - 1, first, second) for n in range(count)]
    for begin in range(0, count, per):
        group = range(begin, min(begin + per, count))
        for tiles in itertools.product(*[options(n) for n in group]):
            fits = [(last[n] >= (t - 1) * 256) & (last[n] < t * 256) for n, t in zip(group, tiles)]

            @pl.when(functools.reduce(jnp.logical_and, fits))
            def _(group=group, tiles=tiles):
                run([item(n, t) for n, t in zip(group, tiles)])


def hide(scores, clear, reach):
    span, block = scores.shape
    places = clear + lax.broadcasted_iota(jnp.int32, (span - clear, block), 0)
    tail = jnp.where(places <= reach, scores[clear:], NEGATIVE)
    return tail if clear == 0 else jnp.concatenate([scores[:clear], tail], axis=0)


def head_masks():
    lanes = lax.broadcasted_iota(jnp.int32, (1, 2 * HEAD_DIM), 1)
    return [lanes < HEAD_DIM, lanes >= HEAD_DIM]


def pick(mask, values):
    return jnp.where(mask, values, jnp.zeros_like(values))


def staggered(count, ahead, start, finish):
    for i in range(min(ahead, count)):
        start(i)
    for i in range(count):
        if i + ahead < count:
            start(i + ahead)
        finish(i)


POWER = SCALE * LOG2E
SAFE = 2.0**100


def attend_body(fixed_offset, starts_ref, offset_ref, q_ref, k_ref, v_ref, out_ref, lse_ref, vt_ref, worst_ref):
    masks = head_masks()
    queries, keys = q_ref.shape[1], k_ref.shape[1]
    pairs = q_ref.shape[2] // 128
    for p in range(pairs):
        vt_ref[p * 128 : (p + 1) * 128, :] = v_ref[0, :, p * 128 : (p + 1) * 128].T
    worst_ref[...] = jnp.zeros_like(worst_ref)

    def run(exact, items):
        units = [(it, p, h) for it in items for p in range(pairs) for h in range(2)]
        held = [None] * len(units)

        def start(i):
            (at, clear, span, reach), p, h = units[i]
            lanes = slice(p * 128, (p + 1) * 128)
            held[i] = hide(dot(k_ref[0, :span, lanes], pick(masks[h], q_ref[0, at, lanes]), NT), clear, reach)

        def finish(i):
            (at, _, span, _), p, h = units[i]
            s = held[i]
            top = jnp.max(s, axis=0, keepdims=True) if exact else s[:1]
            raised = jnp.exp2((s - top) * POWER)
            size = jnp.sum(raised, axis=0, keepdims=True)
            if not exact:
                worst_ref[...] = jnp.maximum(worst_ref[...], size)
            lse_ref[0, p, h : h + 1, at] = top * POWER + jnp.log2(size)
            mine = slice(p * 128 + h * HEAD_DIM, p * 128 + (h + 1) * HEAD_DIM)
            total = dot(vt_ref[mine, :span], raised.astype(BF), NN)
            out_ref[mine, at] = (total * (1.0 / size)).astype(BF)

        staggered(len(units), 2, start, finish)

    args = (starts_ref, offset_ref, queries, keys, fixed_offset)
    query_groups(*args, 2, functools.partial(run, False))

    @pl.when(jnp.max(worst_ref[...]) >= SAFE)
    def _():
        query_groups(*args, 1, functools.partial(run, True))


def attend(starts, offset, q, k, v, fixed_offset):
    count, queries, d = q.shape
    keys = k.shape[1]
    lanes = min(512, d)
    rows = lambda n: pl.BlockSpec((1, n, lanes), lambda b, p, *_: (b, 0, p))
    return pl.pallas_call(
        functools.partial(attend_body, fixed_offset),
        grid_spec=pltpu.PrefetchScalarGridSpec(
            num_scalar_prefetch=2,
            grid=(count, d // lanes),
            in_specs=[rows(queries), rows(keys), rows(keys)],
            out_specs=[
                pl.BlockSpec((lanes, queries), lambda b, p, *_: (p, b)),
                pl.BlockSpec((1, lanes // 128, 2, queries), lambda b, p, *_: (b, p, 0, 0)),
            ],
            scratch_shapes=[pltpu.VMEM((lanes, keys), BF), pltpu.VMEM((1, min(256, queries)), F32)],
        ),
        out_shape=[shape((d, count * queries), BF), shape((count, d // 128, 2, queries), F32)],
        compiler_params=params(),
        cost_estimate=cost(12 * count * queries * keys * d, 8 * count * keys * d, count * d // 64 * queries * keys),
        name="attend",
    )(starts, offset, q, k, v)


def attend_back_body(
    fixed_offset, starts_ref, offset_ref, q_ref, k_ref, v_ref, g_ref, att_ref, lse_ref,
    dq_ref, dkv_ref, kt_ref, settled_ref, dk_acc, dv_acc,
):
    masks = head_masks()
    queries, keys = q_ref.shape[1], k_ref.shape[1]
    pairs = q_ref.shape[2] // 128
    dk_acc[...] = jnp.zeros_like(dk_acc)
    dv_acc[...] = jnp.zeros_like(dv_acc)
    for p in range(pairs):
        lanes = slice(p * 128, (p + 1) * 128)
        kt_ref[lanes, :] = k_ref[0, :, lanes].T
        both = g_ref[0, :, lanes].T.astype(F32) * att_ref[lanes, :].astype(F32)
        for h in range(2):
            part = both[h * HEAD_DIM : (h + 1) * HEAD_DIM]
            settled_ref[2 * p + h : 2 * p + h + 1, :] = jnp.sum(part, axis=0, keepdims=True)

    def run(items):
        units = [(it, p, h) for it in items for p in range(pairs) for h in range(2)]
        held = [None] * len(units)
        done = {}

        def start(i):
            (at, clear, span, reach), p, h = units[i]
            lanes = slice(p * 128, (p + 1) * 128)
            q, g = pick(masks[h], q_ref[0, at, lanes]), pick(masks[h], g_ref[0, at, lanes])
            s = hide(dot(k_ref[0, :span, lanes], q, NT), clear, reach)
            held[i] = (s, dot(v_ref[0, :span, lanes], g, NT), q, g)

        def finish(i):
            (at, _, span, _), p, h = units[i]
            s, chance_grad, q, g = held[i]
            n = 2 * p + h
            chances = jnp.exp2(s * POWER - lse_ref[0, p, h : h + 1, at])
            ds = (chances * (chance_grad - settled_ref[n : n + 1, at])).astype(BF)
            dq = dot(kt_ref[n * HEAD_DIM : (n + 1) * HEAD_DIM, :span], ds, NN)
            done[h] = (chances.astype(BF), ds, q, g, dq)
            if h == 1:
                lanes = slice(p * 128, (p + 1) * 128)
                join = lambda m, axis: jnp.concatenate([done[0][m], done[1][m]], axis=axis)
                dv_acc[:span, lanes] += dot(join(0, 1), join(3, 0), NN)
                dk_acc[:span, lanes] += dot(join(1, 1), join(2, 0), NN)
                dq_ref[0, at, lanes] = (join(4, 0).T * SCALE).astype(BF)

        staggered(len(units), 2, start, finish)

    query_groups(starts_ref, offset_ref, queries, keys, fixed_offset, 2, run)
    dkv_ref[0, 0] = (dk_acc[...] * SCALE).astype(BF)
    dkv_ref[1, 0] = dv_acc[...].astype(BF)


def attend_back(starts, offset, q, k, v, g, att, lse, fixed_offset):
    count, queries, d = q.shape
    keys = k.shape[1]
    lanes = 256
    rows = lambda n: pl.BlockSpec((1, n, lanes), lambda b, p, *_: (b, 0, p))
    return pl.pallas_call(
        functools.partial(attend_back_body, fixed_offset),
        grid_spec=pltpu.PrefetchScalarGridSpec(
            num_scalar_prefetch=2,
            grid=(count, d // lanes),
            in_specs=[
                rows(queries),
                rows(keys),
                rows(keys),
                rows(queries),
                pl.BlockSpec((lanes, queries), lambda b, p, *_: (p, b)),
                pl.BlockSpec((1, lanes // 128, 2, queries), lambda b, p, *_: (b, p, 0, 0)),
            ],
            out_specs=[
                rows(queries),
                pl.BlockSpec((2, 1, keys, lanes), lambda b, p, *_: (0, b, 0, p)),
            ],
            scratch_shapes=[
                pltpu.VMEM((lanes, keys), BF),
                pltpu.VMEM((lanes // HEAD_DIM, queries), F32),
                pltpu.VMEM((keys, lanes), F32),
                pltpu.VMEM((keys, lanes), F32),
            ],
        ),
        out_shape=[shape((count, queries, d), BF), shape((2, count, keys, d), BF)],
        compiler_params=params(),
        cost_estimate=cost(30 * count * queries * keys * d, 14 * count * keys * d, count * d // 64 * queries * keys),
        name="attend_back",
    )(starts, offset, q, k, v, g, att, lse)


def hidden_chunk(up_ref):
    return min(512, up_ref.shape[3])


def up_chunk(up_ref, n, size):
    per = up_ref.shape[3] // size
    block = up_ref[:, n // per, :, (n % per) * size : (n % per + 1) * size]
    return block.reshape(block.shape[0] * block.shape[1], size)


def settle_body(x_ref, att_ref, vec_ref, wo_ref, mid_ref, x2_ref):
    att = att_ref[...]
    parts = [dot(att, weight_columns(wo_ref, j), TN) for j in range(wo_ref.shape[1])]
    branch = jnp.concatenate(parts, axis=1)
    middle = x_ref[...].astype(F32) + (branch + row(vec_ref, OUTPUT_BIAS))
    mid_ref[...] = middle
    hat, _ = norm_parts(middle)
    x2_ref[...] = (hat * row(vec_ref, GAIN_TWO) + row(vec_ref, SHIFT_TWO)).astype(BF)


def settle(x, att, vec, first, tile):
    tokens, d = x.shape
    dp, g, _, width = first.shape
    per = d // dp
    tok = pl.BlockSpec((tile, d), lambda i: (i, 0))
    return pl.pallas_call(
        settle_body,
        grid=(tokens // tile,),
        in_specs=[
            tok,
            pl.BlockSpec((d, tile), lambda i: (0, i)),
            once((8, d), lambda i: (0, 0)),
            once((dp, g, per, width), lambda i: (0, 0, 3, 0)),
        ],
        out_specs=[tok, tok],
        out_shape=[shape((tokens, d), F32), shape((tokens, d), BF)],
        compiler_params=params(),
        cost_estimate=cost(2 * tokens * d * d, 10 * tokens * d + 2 * d * d),
        name="settle",
    )(x, att, vec, first)


def rise_body(x2_ref, upb_ref, up_ref, act_ref, slope_ref):
    x2 = x2_ref[...]
    size = hidden_chunk(up_ref)
    for n in range(up_ref.shape[1] * up_ref.shape[3] // size):
        at = slice(n * size, (n + 1) * size)
        x = dot(x2, up_chunk(up_ref, n, size), NN) + upb_ref[:, at]
        square = x * x
        half = 0.5 + 0.5 * jnp.tanh(x * (BENDING + (BENDING * CUBIC_TERM) * square))
        act_ref[:, at] = (x * half).astype(BF)
        bend = x * (2.0 * BENDING + (6.0 * BENDING * CUBIC_TERM) * square)
        slope_ref[:, at] = (half + half * (1.0 - half) * bend).astype(BF)


def rise(x2, upb, up, tile):
    tokens, d = x2.shape
    ff = upb.shape[1]
    wide = pl.BlockSpec((tile, ff), lambda i: (i, 0))
    return pl.pallas_call(
        rise_body,
        grid=(tokens // tile,),
        in_specs=[
            pl.BlockSpec((tile, d), lambda i: (i, 0)),
            once((1, ff), lambda i: (0, 0)),
            once(up.shape, lambda i: (0, 0, 0, 0)),
        ],
        out_specs=[wide, wide],
        out_shape=[shape((tokens, ff), BF), shape((tokens, ff), BF)],
        compiler_params=params(),
        cost_estimate=cost(2 * tokens * d * ff, tokens * (2 * d + 4 * ff) + 2 * d * ff, tokens * ff),
        name="rise",
    )(x2, upb, up)


def fall_body(
    begun, which_ref, mid_ref, act_ref, slope_ref, og_ref, vec_ref, wo_ref, up_ref, down_ref, *rest
):
    out_ref, bg_ref, mg_ref, br_ref, dat_ref, upb_ref, sums_ref = rest[4:] if begun else rest
    clear_at_start(upb_ref, sums_ref)
    og = og_ref[...]
    incoming = og.astype(F32)
    g, width = down_ref.shape[1], down_ref.shape[3]
    size = hidden_chunk(up_ref)
    per = size // down_ref.shape[2]
    chunks = up_ref.shape[1] * up_ref.shape[3] // size
    outs = [None] * g
    e = None
    for n in range(chunks):
        at = slice(n * size, (n + 1) * size)
        act = act_ref[:, at]
        rise_grad = None
        for j in range(g):
            block = down_ref[n * per : (n + 1) * per, j].reshape(size, width)
            part = dot(og[:, j * width : (j + 1) * width], block, NT)
            rise_grad = part if rise_grad is None else rise_grad + part
            part = dot(act, block, NN)
            outs[j] = part if outs[j] is None else outs[j] + part
        bg = (slope_ref[:, at].astype(F32) * rise_grad).astype(BF)
        bg_ref[:, at] = bg
        upb_ref[:, at] += fold(bg.astype(F32))
        part = dot(bg, up_chunk(up_ref, n, size), NT)
        e = part if e is None else e + part
    middle = mid_ref[...]
    out_ref[...] = (middle + (jnp.concatenate(outs, axis=1) + row(vec_ref, DOWN_BIAS))).astype(BF)
    hat, inverse = norm_parts(middle)
    middle_grad = incoming + norm_back(e, hat, inverse, row(vec_ref, GAIN_TWO))
    mg_ref[...] = middle_grad
    branch = middle_grad.astype(BF)
    br_ref[...] = branch
    back = None
    for j in range(wo_ref.shape[1]):
        part = dot(branch[:, j * width : (j + 1) * width], weight_columns(wo_ref, j), NT)
        back = part if back is None else back + part
    dat_ref[...] = back.astype(BF)
    sums_ref[0] += fold(e * hat)
    sums_ref[1] += fold(e)
    sums_ref[2] += fold(branch.astype(F32))
    sums_ref[3] += fold(incoming)


def fall(middle, act, slope, og, vec, first, up, down, tile, which, sequences, halves, begun=()):
    tokens, d = og.shape
    dp, g, _, width = first.shape
    per = d // dp
    ff = act.shape[1]
    per_half = tokens // tile // sequences // halves
    kept = tokens // halves

    def block(i, w):
        return (i // per_half) * (per_half * halves) + w[0] * per_half + i % per_half, 0

    tok = pl.BlockSpec((tile, d), block)
    wide = pl.BlockSpec((tile, ff), block)
    fixed = lambda dims: once(dims, lambda i, w: (0,) * len(dims))
    return pl.pallas_call(
        functools.partial(fall_body, bool(begun)),
        grid_spec=pltpu.PrefetchScalarGridSpec(
            num_scalar_prefetch=1,
            grid=(kept // tile,),
            in_specs=[
                tok, wide, wide, tok,
                fixed((8, d)),
                once((dp, g, per, width), lambda i, w: (0, 0, 3, 0)),
                fixed(up.shape),
                fixed(down.shape),
            ] + [pl.BlockSpec(memory_space=pl.ANY)] * len(begun),
            out_specs=[
                pl.BlockSpec((tile, d), lambda i, w: (i, 0)), wide, tok, tok, tok,
                pl.BlockSpec((8, ff), lambda i, w: (0, 0)),
                pl.BlockSpec((4, 8, d), lambda i, w: (0, 0, 0)),
            ],
        ),
        out_shape=[
            shape((kept, d), BF), shape((tokens, ff), BF), shape((tokens, d), F32), shape((tokens, d), BF),
            shape((tokens, d), BF), shape((8, ff), F32), shape((4, 8, d), F32),
        ],
        input_output_aliases={9 + n: 1 + n for n in range(len(begun))},
        compiler_params=params(),
        cost_estimate=cost(2 * kept * d * (d + 3 * ff), kept * (16 * d + 6 * ff) + 2 * d * (d + 2 * ff)),
        name="fall",
    )(which, middle, act, slope, og, vec, first, up, down, *begun)


def split_cores(core_ref, values, keep_ref, send_ref):
    even, odd = values[:, 0], values[:, 1]
    mine = core_ref[0] == 0
    keep_ref[...] = jnp.where(mine, even, odd).astype(BF)
    send_ref[...] = jnp.where(mine, odd, even).astype(BF)


def down_grad_body(core_ref, act_ref, og_ref, keep_ref, send_ref):
    y = dot(act_ref[...], og_ref[...], TN)
    chips, g, rows, width = keep_ref.shape
    for j in range(g):
        part = y[:, j * width : (j + 1) * width].reshape(chips, 2, rows, width)
        split_cores(core_ref, part, keep_ref.at[:, j], send_ref.at[:, j])


def down_grad(core, act, og, dp, g):
    tokens, ff = act.shape
    d = og.shape[1]
    size = min(512, ff)
    rows, width = ff // dp, d // g
    chips = size // rows // 2
    out = pl.BlockSpec((chips, g, rows, width), lambda i, *_: (i, 0, 0, 0))
    return pl.pallas_call(
        down_grad_body,
        grid_spec=pltpu.PrefetchScalarGridSpec(
            num_scalar_prefetch=1,
            grid=(ff // size,),
            in_specs=[pl.BlockSpec((tokens, size), lambda i, *_: (0, i)), once((tokens, d), lambda i, *_: (0, 0))],
            out_specs=[out, out],
        ),
        out_shape=[shape((dp // 2, g, rows, width), BF)] * 2,
        compiler_params=params(),
        cost_estimate=cost(2 * tokens * d * ff, 2 * (tokens * (d + ff) + d * ff)),
        name="down_grad",
    )(core, act, og)


def weight_grad_body(form, core_ref, x_ref, dy_ref, keep_ref, send_ref):
    dy = dy_ref[...]
    y = dot(x_ref[...], dy.reshape(dy.shape[-2:]), form)
    chips, _, rows, width = keep_ref.shape
    split_cores(core_ref, y.reshape(chips, 2, rows, width), keep_ref.at[:, 0], send_ref.at[:, 0])


def weight_grad(core, x, dy, dp, g, form, name):
    count, tokens, columns = dy.shape
    d = x.shape[0] if form == NN else x.shape[1]
    share = columns // g
    size = min(512, share)
    per = share // size
    rows = d // dp
    out = pl.BlockSpec((dp // 2, 1, rows, size), lambda m, i, *_: (0, i // per, m, i % per))
    return pl.pallas_call(
        functools.partial(weight_grad_body, form),
        grid_spec=pltpu.PrefetchScalarGridSpec(
            num_scalar_prefetch=1,
            grid=(count, columns // size),
            in_specs=[
                once(x.shape, lambda m, i, *_: (0, 0)),
                pl.BlockSpec((1, tokens, size), lambda m, i, *_: (m, 0, i)),
            ],
            out_specs=[out, out],
        ),
        out_shape=[shape((dp // 2, g, count * rows, share), BF)] * 2,
        compiler_params=params(),
        cost_estimate=cost(2 * count * tokens * d * columns, 2 * (tokens * d + count * columns * (tokens + d))),
        name=name,
    )(core, x, dy)


def input_body(which_ref, x_ref, mg_ref, dq_ref, dkv_ref, vec_ref, w_ref, out_ref, sums_ref):
    clear_at_start(sums_ref)
    groups, per, width = w_ref.shape[1], w_ref.shape[2] // 3, w_ref.shape[3]
    e = None
    grads = (dq_ref[...], dkv_ref[0], dkv_ref[1])
    for m in range(3):
        for j in range(groups):
            at = slice(j * width, (j + 1) * width)
            part = dot(grads[m][:, at], weight_columns(w_ref, j, slice(m * per, (m + 1) * per)), NT)
            e = part if e is None else e + part
    hat, inverse = norm_parts(x_ref[...].astype(F32))
    out_ref[...] = (mg_ref[...] + norm_back(e, hat, inverse, row(vec_ref, GAIN_ONE))).astype(BF)
    sums_ref[0] += fold(e * hat)
    sums_ref[1] += fold(e)
    sums_ref[2] += fold(grads[0].astype(F32))
    sums_ref[3] += fold(grads[2].astype(F32))


def input_back(x, mg, dq, dkv, vec, first, tile, which, sequences, halves):
    tokens, d = x.shape
    dp, g, rows, width = first.shape
    per = d // dp
    per_half = tokens // tile // sequences // halves

    def block(i, which):
        return (i // per_half) * (per_half * halves) + which[0] * per_half + i % per_half

    tok = pl.BlockSpec((tile, d), lambda i, w: (block(i, w), 0))
    kept = tokens // halves
    return pl.pallas_call(
        input_body,
        grid_spec=pltpu.PrefetchScalarGridSpec(
            num_scalar_prefetch=1,
            grid=(kept // tile,),
            in_specs=[
                tok, tok, tok,
                pl.BlockSpec((2, tile, d), lambda i, w: (0, block(i, w), 0)),
                once((8, d), lambda i, w: (0, 0)),
                once((dp, g, 3 * per, width), lambda i, w: (0, 0, 0, 0)),
            ],
            out_specs=[
                pl.BlockSpec((tile, d), lambda i, w: (i, 0)),
                pl.BlockSpec((4, 8, d), lambda i, w: (0, 0, 0)),
            ],
        ),
        out_shape=[shape((kept, d), BF), shape((4, 8, d), F32)],
        compiler_params=params(),
        cost_estimate=cost(6 * kept * d * d, 16 * kept * d + 6 * d * d),
        name="input_back",
    )(which, x, mg, dq, dkv, vec, first)


def swap_cores(values):
    return lax.ppermute(values, "core", [(0, 1), (1, 0)])


def add_cores(keep, send):
    return (keep.astype(F32) + swap_cores(send).astype(F32)).astype(BF)


def add_chips(mine):
    chips, g = mine.shape[:2]
    flat = mine.reshape((chips * g,) + mine.shape[2:])
    return lax.psum_scatter(flat, ("z", "x", "seq"), scatter_dimension=0, tiled=True)[0].astype(F32)


NEAR = ("z", [(0, 1), (1, 0), (2, 3), (3, 2)])
FAR = ("z", [(0, 2), (2, 0), (1, 3), (3, 1)])
ACROSS = ("x", [(0, 1), (1, 0)])
ALONG = ("seq", [(0, 1), (1, 0)])


def cut(values, dim, own, route):
    keep = lax.dynamic_index_in_dim(values, own, dim, keepdims=False)
    return keep, lax.dynamic_index_in_dim(values, 1 - own, dim, keepdims=False), route


def add_step(step, came):
    return (step[0].astype(F32) + came.astype(F32)).astype(BF)


def halve(values, dim, own, route):
    step = cut(values, dim, own, route)
    return add_step(step, lax.ppermute(step[1], *route))


def start_step(mine, across_first):
    values = mine.reshape((2, 2, 2) + mine.shape[1:])
    if across_first:
        return cut(values, 2, lax.axis_index("x"), ACROSS)
    return cut(values, 1, lax.axis_index("z") % 2, NEAR)


def next_step(values, across_first):
    if across_first:
        return cut(values, 1, lax.axis_index("z") % 2, NEAR)
    return cut(values, 0, lax.axis_index("z") // 2, FAR)


def last_steps(values, across_first):
    if across_first:
        values = halve(values, 0, lax.axis_index("z") // 2, FAR)
    else:
        values = halve(values, 0, lax.axis_index("x"), ACROSS)
    return halve(values, 0, lax.axis_index("seq"), ALONG).astype(F32)


def all_steps(mine):
    step = start_step(mine, True)
    step = next_step(add_step(step, lax.ppermute(step[1], *step[2])), True)
    return last_steps(add_step(step, lax.ppermute(step[1], *step[2])), True)


def body(
    tokens, first_gain, first_shift, query_weight, query_bias, key_weight, value_weight, value_bias,
    output_weight, output_bias, second_gain, second_shift, up_weight, up_bias, down_weight, down_bias,
    piece_starts, out_grad,
):
    chips, g = lax.axis_size("z") * lax.axis_size("x"), lax.axis_size("seq")
    dp = 2 * chips
    everyone = ("z", "x", "core", "seq")
    count, local, d = tokens.shape
    width = query_weight.shape[1]
    per = query_weight.shape[0]
    small = first_gain.shape[0]
    wide = up_bias.shape[0]
    ff = wide * dp * g
    length = local * g
    place = lax.axis_index("seq")
    core = lax.axis_index("core").astype(jnp.int32).reshape(1)
    paired = g == 2 and count % 2 == 0

    vectors = [first_gain, first_shift, query_bias, value_bias, output_bias, second_gain, second_shift, down_bias]
    extra = 16
    packed = pack([query_weight, key_weight, value_weight, output_weight], vectors + [up_bias], extra)
    first = lax.all_gather(packed, everyone, axis=0).reshape(dp, g, 4 * per + extra, width)
    up = lax.all_gather(up_weight, everyone, axis=0).reshape((dp, g) + up_weight.shape)
    down = lax.all_gather(down_weight, everyone, axis=0).reshape((dp, g) + down_weight.shape)

    if paired:
        half = count // 2

        def swap_rows(values, *earlier):
            sent = lax.dynamic_slice_in_dim(values, (1 - place) * half, half, 0)
            return lax.ppermute(after(sent, *earlier), "seq", [(0, 1), (1, 0)])

        def gather_rows(values, came):
            kept = lax.dynamic_slice_in_dim(values, place * half, half, 0)
            low = jnp.where(place == 0, kept, came)
            high = jnp.where(place == 0, came, kept)
            return jnp.concatenate([low, high], axis=1).reshape(half * length, d)

        def join_rows(kept, came):
            low = jnp.where(place == 0, kept, came)
            high = jnp.where(place == 0, came, kept)
            return jnp.concatenate([low, high], axis=0)

        starts = lax.dynamic_slice_in_dim(piece_starts, place * half, half, 0)
        offset = jnp.zeros((1,), jnp.int32)
        sequences, queries = half, length
    else:
        swap_rows = lambda values, *earlier: values
        gather_rows = lambda values, came: values.reshape(count * local, d)
        starts = piece_starts
        offset = (place * local).astype(jnp.int32).reshape(1)
        sequences, queries = count, local

    rows = sequences * queries
    tile = min(256, rows)
    x = gather_rows(tokens, swap_rows(tokens))
    first = after(first, x)
    vec = first[:, :, 4 * per : 4 * per + 8, :small].astype(F32).transpose(2, 0, 1, 3).reshape(8, d)
    upb = first[:, :, 4 * per + 8, :wide].astype(F32).reshape(1, ff)
    came = swap_rows(out_grad, first)
    x1, q, k, v = project(x, vec, first, min(512, rows))
    q, k, v = (t.reshape(sequences, queries, d) for t in (q, k, v))
    if not paired:
        k, v = (lax.all_gather(t, "seq", axis=1, tiled=True) for t in (k, v))
    att, lse = attend(starts, offset, q, k, v, paired)
    og = gather_rows(out_grad, after(came, att))
    middle, x2 = settle(x, att, vec, first, min(512, rows))
    act, slope = rise(after(x2, og), upb, up, min(512, rows))
    down_mine = add_cores(*down_grad(core, act, og, dp, g))
    down_sum = add_chips(down_mine)
    act = after(act, down_mine)
    args = (middle, act, slope, og, vec, first, up, down, tile)
    if paired:
        turn = place.astype(jnp.int32).reshape(1)
        out_sent, *begun, upb_sent, two_sent = fall(*args, 1 - turn, sequences, 2)
        out, *begun, upb_sums, sums_two = fall(*args, turn, sequences, 2, tuple(begun))
        bg, mg, branch, dat = begun
        upb_sums, sums_two = upb_sums + upb_sent, sums_two + two_sent
        came_out = lax.ppermute(out_sent.reshape(half, local, d), *ALONG)
    else:
        out, bg, mg, branch, dat, upb_sums, sums_two = fall(*args, jnp.zeros((1,), jnp.int32), sequences, 1)
        output = out.reshape(count, local, d)
    up_parts = weight_grad(core, x2, bg[None], dp, g, TN, "up_grad")
    out_parts = weight_grad(core, att, branch[None], dp, g, NN, "out_grad")
    if paired:
        up_parts, out_parts, came_out = lax.optimization_barrier((up_parts, out_parts, came_out))
        output = join_rows(out.reshape(half, local, d), came_out)
    up_mine = jnp.concatenate([add_cores(*up_parts), add_cores(*out_parts)], axis=-1)
    up_sum = add_chips(up_mine)
    dat = after(dat, up_mine, down_sum)
    dq, dkv = attend_back(starts, offset, q, k, v, dat.reshape(sequences, queries, d), att, lse, paired)
    dq = dq.reshape(rows, d)
    if not paired:
        dkv = lax.psum_scatter(dkv, "seq", scatter_dimension=2, tiled=True)
    dkv = dkv.reshape(2, rows, d)
    query_parts = weight_grad(core, x1, dq[None], dp, g, TN, "query_grad")
    kv_parts = weight_grad(core, x1, dkv, dp, g, TN, "key_value_grad")
    query_mine, kv_mine = add_cores(*query_parts), add_cores(*kv_parts)
    first_parts = jnp.concatenate([query_mine, kv_mine[:, :, :per]], axis=2)
    second_parts = kv_mine[:, :, per:]
    stepwise = (lax.axis_size("z"), lax.axis_size("x"), g) == (4, 2, 2)
    dkv = after(dkv, first_parts, second_parts, up_sum)
    args = (x, mg, dq, dkv, vec, first, tile)
    if paired:
        sent, sums_sent = input_back(*args, 1 - turn, sequences, 2)
        came_in = lax.ppermute(sent.reshape(half, local, d), *ALONG)
        if stepwise:
            steps = [start_step(first_parts, True), start_step(second_parts, False)]
            arrived = [after(lax.ppermute(move, *route), sent) for _, move, route in steps]
            steps = [next_step(add_step(step, move), n == 0) for n, (step, move) in enumerate(zip(steps, arrived))]
            arrived = [lax.ppermute(move, *route) for _, move, route in steps]
            args = args[:3] + (after(dkv, steps[0][1], steps[1][1]),) + args[4:]
        in_grad, sums_one = input_back(*args, turn, sequences, 2)
        if stepwise:
            arrived[0], arrived[1], came_in, sums_one = lax.optimization_barrier((*arrived, came_in, sums_one))
            summed = [add_step(step, move) for step, move in zip(steps, arrived)]
        sums_one = sums_one + sums_sent
        came_in = lax.ppermute(sent.reshape(half, local, d), "seq", [(0, 1), (1, 0)])
        input_grad = join_rows(in_grad.reshape(half, local, d), came_in)
    else:
        in_grad, sums_one = input_back(*args, jnp.zeros((1,), jnp.int32), sequences, 1)
        input_grad = in_grad.reshape(count, local, d)

    one, two = jnp.sum(sums_one, axis=1), jnp.sum(sums_two, axis=1)
    eight = jnp.stack([one[0], one[1], one[2], one[3], two[2], two[0], two[1], two[3]])
    eight = eight.reshape(8, chips, 2, g, small).transpose(2, 1, 3, 0, 4).reshape(2, chips, g, 8 * small)
    upb_grad = jnp.sum(upb_sums, axis=0).reshape(chips, 2, g, wide).transpose(1, 0, 2, 3)
    lines = jnp.concatenate([eight, upb_grad], axis=-1)
    lines = jnp.pad(lines, ((0, 0), (0, 0), (0, 0), (0, extra * width - lines.shape[-1])))
    lines = lines.reshape(2, chips, g, extra, width).astype(BF)
    own = lax.axis_index("core")
    line_mine = add_cores(
        lax.dynamic_index_in_dim(lines, own, 0, keepdims=False),
        lax.dynamic_index_in_dim(lines, 1 - own, 0, keepdims=False),
    )
    if stepwise:
        last = [last_steps(summed[0], True), last_steps(summed[1], False), all_steps(line_mine)]
        last = jnp.concatenate(last, axis=0)
    else:
        last = add_chips(jnp.concatenate([first_parts, second_parts, line_mine], axis=2))
    dw = [last[m * per : (m + 1) * per] for m in range(3)] + [up_sum[:, -width:]]
    up_sum = up_sum[:, :-width]
    line = last[3 * per :].reshape(extra * width)
    grads = [line[m * small : (m + 1) * small] for m in range(8)]
    gain_one, shift_one, query_add, value_add, output_add, gain_two, shift_two, down_add = grads
    up_add = line[8 * small : 8 * small + wide]
    return (
        output, input_grad, gain_one, shift_one, dw[0], query_add, dw[1], dw[2], value_add, dw[3], output_add,
        gain_two, shift_two, up_sum, up_add, down_sum, down_add,
    )


def solution(mesh):
    dp, g = mesh.shape["dp"], mesh.shape["seq"]
    fine = Mesh(mesh.devices.reshape(4, dp // 8, 2, g), ("z", "x", "core", "seq"))
    both = ("z", "x", "core")
    rows, vector, matrix = P(both, "seq", None), P(both + ("seq",)), P(both, "seq")
    in_specs = (
        rows, vector, vector, matrix, vector, matrix, matrix, vector, matrix, vector, vector, vector, matrix,
        vector, matrix, vector, P(both, None), rows,
    )
    out_specs = (
        rows, rows, vector, vector, matrix, vector, matrix, matrix, vector, matrix, vector, vector, vector,
        matrix, vector, matrix, vector,
    )
    return jax.shard_map(body, mesh=fine, in_specs=in_specs, out_specs=out_specs, check_vma=False)
```
